256 devices in a mesh: head: 4 (over x), ctx: 64 (over z, y, core).
Axes of the slice: x: 4, y: 4, z: 8, core: 2. Of those that a mesh axis runs over, the one named last changes fastest.
Arguments:
- query: bfloat16 [256, 384, 3072], P('ctx', 'head'), may hold values from -6 to 6
- keys_in: bfloat16 [256, 384, 3072], P('ctx', 'head'), may hold values from -6 to 6
- values_in: bfloat16 [256, 384, 3072], P('ctx', 'head'), may hold values from -6 to 6
- pair_keys: int32 [256, 8], P('ctx'), may hold values from 0 to 255, as said below
- pair_count: int32 [256], P('ctx'), may hold values from 1 to 8
Outputs:
- attended: bfloat16 [256, 384, 3072], P('ctx', 'head')
The draws below stay inside these ranges and needn't reach their ends.
Inputs may be any that keep to these rules, and one draw needn't show every extreme that they name: `pair_keys`: entry 0 of row t is t itself; entries 0 to pair_count[t] - 1 are distinct; every entry of row t, used or not, names a tile whose ctx index differs from that of t by at most 1; entries from pair_count[t] on are ignored.
All inputs are finite; a program needn't handle non-finite values.
Results may differ from the reference program's by a relative error of at most 0.0045.
Values may be sent and summed in bfloat16 or wider, within the bound.
A program may use at most 128 MiB of HBM per device.

```python
import jax
import jax.numpy as jnp
from jax import lax

HEADS = 24
DH = 128
TILE_TOK = 384
TILE_DEV = 4
REACH = 1
MOST = 8
TILES = 256
HD = 3072


def pair_pattern(key):
    counts = jax.random.randint(jax.random.fold_in(key, 101), (TILES,), 1, MOST + 1)
    first_pick = jax.random.randint(jax.random.fold_in(key, 102), (), 0, TILES)
    second_pick = (first_pick + 1 + jax.random.randint(jax.random.fold_in(key, 103), (), 0, TILES - 1)) % TILES
    counts = counts.at[first_pick].set(MOST)
    counts = counts.at[second_pick].set(1)
    slots = jnp.arange(TILES)
    owners = slots // TILE_DEV
    wide = (2 * REACH + 1) * TILE_DEV
    offsets = jnp.arange(wide)
    candidates = owners[:, None] * TILE_DEV - REACH * TILE_DEV + offsets[None, :]
    usable = (candidates >= 0) & (candidates < TILES) & (candidates != slots[:, None])
    noise = jax.random.randint(jax.random.fold_in(key, 104), (TILES, wide), 0, 1 << 20)
    ranks = jnp.where(usable, noise * 64 + offsets[None, :], (1 << 28) + offsets[None, :])
    order = jnp.argsort(ranks, axis=1, stable=True)[:, :MOST - 1]
    others = jnp.take_along_axis(candidates, order, axis=1)
    listed = jnp.concatenate([slots[:, None], others], axis=1)
    return (listed.astype(jnp.int32), counts.astype(jnp.int32))


def aligned_fields(key, boost):
    shape = (TILES, TILE_TOK // 2, 2, HEADS, DH)
    queries = jnp.clip(jax.random.normal(jax.random.fold_in(key, 201), shape, jnp.float32), -6.0, 6.0)
    keyset = jnp.clip(jax.random.normal(jax.random.fold_in(key, 202), shape, jnp.float32), -6.0, 6.0)
    picked = jax.random.randint(jax.random.fold_in(key, 203), (TILES, TILE_TOK // 2, 1, 1, 1), 0, 24) == 0
    levels = jax.random.randint(jax.random.fold_in(key, 204), (TILES, TILE_TOK // 2, 1, 1, 1), 0, 3)
    factor = 0.75 + 0.125 * levels.astype(jnp.float32)
    signs = jnp.where(jax.random.normal(jax.random.fold_in(key, 205), (TILES, TILE_TOK // 2, 1, HEADS, DH)) > 0, 1.0, -1.0) * boost
    damped = jnp.where(jnp.arange(DH) == 0, 0.2, 1.0)
    key_pair = jnp.concatenate([signs, signs * damped], axis=2)
    query_pair = jnp.concatenate([factor * signs, queries[:, :, 1:2]], axis=2)
    active = picked & (boost > 0)
    keyset = jnp.where(active, key_pair, keyset)
    queries = jnp.where(active, query_pair, queries)
    return (queries.reshape(TILES, TILE_TOK, HEADS * DH), keyset.reshape(TILES, TILE_TOK, HEADS * DH))


def draw_query(key, part):
    boost = 0.0
    return aligned_fields(key, boost)[0].astype(jnp.bfloat16)


def draw_keys_in(key, part):
    boost = 0.0
    return aligned_fields(key, boost)[1].astype(jnp.bfloat16)


def draw_pair_keys(key, part):
    return pair_pattern(key)[0]


def draw_pair_count(key, part):
    return pair_pattern(key)[1]


def block_scale(rng, shape, split, smallest, largest):
    level, own = 1.0, jax.random.fold_in(rng, 6)
    for axis_at, shards_of in split:
        steps = jnp.exp(jax.random.uniform(jax.random.fold_in(own, axis_at), (shards_of,), jnp.float32, smallest / len(split), largest / len(split)))
        level = level * jnp.repeat(steps, shape[axis_at] // shards_of).reshape([-1 if axis == axis_at else 1 for axis in range(len(shape))])
    return level


def normal_values(stream_key, extent, spread, bound, shards=(), held_as=jnp.bfloat16):
    entries = jax.random.normal(stream_key, extent, jnp.float32) * spread
    if len(shards) > 0:
        entries = block_scale(stream_key, extent, shards, -0.22, 0.18) * entries
    return jnp.clip(entries, min=-bound, max=bound).astype(held_as)


def setup_inputs(seed: int = 0) -> dict:
    splits = jax.random.split(jax.random.key(seed), 6)
    query = draw_query(jax.random.fold_in(splits[5], 71), 0)
    keys_in = draw_keys_in(jax.random.fold_in(splits[5], 71), 0)
    values_in = normal_values(splits[2], (TILES, TILE_TOK, HD), 1.0, 6.0, ((0, 64), (1, 4)))
    pair_keys = draw_pair_keys(jax.random.fold_in(splits[5], 71), 0)
    pair_count = draw_pair_count(jax.random.fold_in(splits[5], 71), 0)
    return {"query": query, "keys_in": keys_in, "values_in": values_in, "pair_keys": pair_keys, "pair_count": pair_count}


def reference(query, keys_in, values_in, pair_keys, pair_count):
    score_scale = DH ** -0.5

    def one_tile(t):
        query_tile = query[t].astype(jnp.float32).reshape(TILE_TOK, HEADS, DH)
        live_count = pair_count[t]
        maxima = []
        totals = []
        partial_outs = []
        for p in range(MOST):
            key_slot = pair_keys[t, p]
            keys_tile = keys_in[key_slot].astype(jnp.float32).reshape(TILE_TOK, HEADS, DH)
            values_tile = values_in[key_slot].astype(jnp.float32).reshape(TILE_TOK, HEADS, DH)
            scores = jnp.einsum('qhd,khd->qhk', query_tile, keys_tile) * score_scale
            tile_max = jnp.max(scores, axis=-1)
            expo = jnp.exp(scores - tile_max[..., None])
            tile_sum = jnp.sum(expo, axis=-1)
            weights = lax.optimization_barrier(expo.astype(jnp.bfloat16)).astype(jnp.float32)
            tile_out = jnp.einsum('qhk,khd->qhd', weights, values_tile)
            is_pair = p < live_count
            maxima.append(jnp.where(is_pair, tile_max, jnp.float32(-1e30)))
            totals.append(tile_sum)
            partial_outs.append(tile_out)
        top = jnp.max(jnp.stack(maxima), axis=0)
        numer = jnp.zeros((TILE_TOK, HEADS, DH), jnp.float32)
        denom = jnp.zeros((TILE_TOK, HEADS), jnp.float32)
        for p in range(MOST):
            factor = jnp.exp(maxima[p] - top)
            numer = numer + factor[..., None] * partial_outs[p]
            denom = denom + factor * totals[p]
        return (numer / denom[..., None]).reshape(TILE_TOK, HEADS * DH).astype(jnp.bfloat16)

    return lax.map(one_tile, jnp.arange(TILES))
```

```python
import jax
import jax.numpy as jnp
from jax import lax
from jax.experimental import pallas as pl
from jax.experimental.pallas import tpu as pltpu
from jax.sharding import PartitionSpec as P

DH = 128
GROUP = 4
EXP2_SCALE = DH ** -0.5 * 1.4426950408889634
MASKED = 1e30
MESH = pl.DeviceIdType.MESH


def build_kernel(n_head, n_ctx, tiles, rows, heads, most):
    tok = n_head * rows

    def kernel(slots_ref, count_ref, q_ref, k_ref, v_ref, out_ref, *scratch):
        kwin, vwin = scratch[:heads], scratch[heads:2 * heads]
        q_all, v_all, o_all, rx, tx, win, wtx, o_rx, o_tx = scratch[2 * heads:]
        me_h, me_c = lax.axis_index("head"), lax.axis_index("ctx")
        first_slot = (me_c - 1) * tiles
        up, down = lax.rem(me_c + 1, n_ctx), lax.rem(me_c + n_ctx - 1, n_ctx)
        others = [lax.rem(me_h + step, n_head) for step in (1, n_head - 1, *range(2, n_head - 1))]

        barrier = pltpu.get_barrier_semaphore()
        for other in others:
            pl.semaphore_signal(barrier, inc=1, device_id={"head": other}, device_id_type=MESH)
        for other in (up, down):
            pl.semaphore_signal(barrier, inc=1, device_id={"ctx": other}, device_id_type=MESH)
        pl.semaphore_wait(barrier, len(others) + 2)

        def head_columns(owner, g):
            return pl.ds(pl.multiple_of((owner * heads + g) * DH, DH), DH)

        def token_rows(owner):
            return pl.ds(pl.multiple_of(owner * rows, rows), rows)

        def landing(which, g):
            if which == 0:
                return kwin[g].at[tiles:2 * tiles]
            return (v_all if which == 1 else q_all).at[g]

        def send_inputs(g):
            for which, source in enumerate((k_ref, v_ref, q_ref)):
                target = landing(which, g).at[:, token_rows(me_h), :]
                for other in others:
                    pltpu.make_async_remote_copy(
                        src_ref=source.at[:, :, head_columns(other, g)],
                        dst_ref=target,
                        send_sem=tx.at[which],
                        recv_sem=rx.at[which, g],
                        device_id={"head": other},
                        device_id_type=MESH,
                    ).start()
                pltpu.make_async_copy(
                    source.at[:, :, head_columns(me_h, g)], target, rx.at[which, g]
                ).start()

        def await_bytes(ref, sem):
            pltpu.make_async_copy(ref, ref, sem).wait()

        def send_window(which, window, g):
            for other, place in ((up, 0), (down, 2 * tiles)):
                pltpu.make_async_remote_copy(
                    src_ref=window[g].at[tiles:2 * tiles],
                    dst_ref=window[g].at[place:place + tiles],
                    send_sem=wtx.at[which, g],
                    recv_sem=win.at[which, g],
                    device_id={"ctx": other},
                    device_id_type=MESH,
                ).start()

        def share(g):
            await_bytes(landing(0, g), rx.at[0, g])
            send_window(0, kwin, g)
            await_bytes(landing(1, g), rx.at[1, g])

            def turn(t, carry):
                vwin[g][tiles + t] = v_all[g, t].T
                return carry

            lax.fori_loop(0, tiles, turn, 0)
            send_window(1, vwin, g)

        def compute(g):
            def one_tile(t, carry):
                query_t = q_all[g, t].T
                live = count_ref[t]
                top = jnp.full((1, tok), -MASKED, jnp.float32)
                total = jnp.zeros((1, tok), jnp.float32)
                out_t = jnp.zeros((DH, tok), jnp.float32)
                for base in range(0, most, GROUP):
                    scores, values, shifts = [], [], []
                    new_top = top
                    for p in range(base, base + GROUP):
                        slot = jnp.clip(slots_ref[t, p] - first_slot, 0, 3 * tiles - 1)
                        s = jnp.dot(kwin[g][slot], query_t, preferred_element_type=jnp.float32)
                        shift = jnp.where(p < live, 0.0, MASKED).astype(jnp.float32)
                        new_top = jnp.maximum(new_top, jnp.max(s, axis=0, keepdims=True) - shift)
                        scores.append(s)
                        values.append(vwin[g][slot])
                        shifts.append(shift)
                    top_scaled = new_top * EXP2_SCALE
                    old_factor = jnp.exp2(top * EXP2_SCALE - top_scaled)
                    total = total * old_factor
                    out_t = out_t * old_factor
                    for i in range(0, GROUP, 2):
                        weights = []
                        for s, shift in zip(scores[i:i + 2], shifts[i:i + 2]):
                            expo = jnp.exp2(s * EXP2_SCALE - (top_scaled + shift))
                            total = total + jnp.sum(expo, axis=0, keepdims=True)
                            weights.append(expo.astype(jnp.bfloat16))
                        out_t = out_t + jnp.dot(
                            jnp.concatenate(values[i:i + 2], axis=1),
                            jnp.concatenate(weights, axis=0),
                            preferred_element_type=jnp.float32,
                        )
                    top = new_top
                o_all[g, t] = (out_t / total).T.astype(jnp.bfloat16)
                return carry

            lax.fori_loop(0, tiles, one_tile, 0)

        def send_outputs(g):
            target = out_ref.at[:, :, head_columns(me_h, g)]
            for other in others:
                pltpu.make_async_remote_copy(
                    src_ref=o_all.at[g, :, token_rows(other), :],
                    dst_ref=target,
                    send_sem=o_tx.at[g],
                    recv_sem=o_rx.at[g],
                    device_id={"head": other},
                    device_id_type=MESH,
                ).start()
            pltpu.make_async_copy(
                o_all.at[g, :, token_rows(me_h), :], target, o_rx.at[g]
            ).start()

        send_inputs(0)
        if heads > 1:
            send_inputs(1)
        share(0)
        for g in range(heads):
            if g + 2 < heads:
                send_inputs(g + 2)
            if g + 1 < heads:
                share(g + 1)
            await_bytes(q_all.at[g], rx.at[2, g])
            await_bytes(kwin[g].at[:2 * tiles], win.at[0, g])
            await_bytes(vwin[g].at[:2 * tiles], win.at[1, g])
            compute(g)
            send_outputs(g)

        sent = tiles * (n_head - 1) // n_head
        for which, source in enumerate((k_ref, v_ref, q_ref)):
            await_bytes(source.at[:sent], tx.at[which])
        for g in range(heads):
            await_bytes(kwin[g].at[:2 * tiles], wtx.at[0, g])
            await_bytes(vwin[g].at[:2 * tiles], wtx.at[1, g])
            await_bytes(o_all.at[g, :, :(n_head - 1) * rows, :], o_tx.at[g])
            await_bytes(o_all.at[g], o_rx.at[g])

    return kernel


def solution(mesh):
    n_head, n_ctx = mesh.shape["head"], mesh.shape["ctx"]

    def body(query, keys_in, values_in, pair_keys, pair_count):
        tiles, rows, width = query.shape
        most = pair_keys.shape[1]
        tok, heads = rows * n_head, width // DH // n_head
        units = tiles * most * heads
        dma = pltpu.SemaphoreType.DMA
        scratch = [pltpu.VMEM((3 * tiles, tok, DH), jnp.bfloat16)] * heads
        scratch += [pltpu.VMEM((3 * tiles, DH, tok), jnp.bfloat16)] * heads
        scratch += [pltpu.VMEM((heads, tiles, tok, DH), jnp.bfloat16)] * 3
        scratch += [dma((3, heads)), dma((3,)), dma((2, heads)), dma((2, heads)), dma((heads,)), dma((heads,))]
        smem = pl.BlockSpec(memory_space=pltpu.SMEM)
        anywhere = pl.BlockSpec(memory_space=pl.ANY)
        return pl.pallas_call(
            build_kernel(n_head, n_ctx, tiles, rows, heads, most),
            out_shape=jax.ShapeDtypeStruct(query.shape, query.dtype),
            in_specs=[smem, smem, anywhere, anywhere, anywhere],
            out_specs=anywhere,
            scratch_shapes=scratch,
            compiler_params=pltpu.CompilerParams(
                collective_id=0, has_side_effects=True, vmem_limit_bytes=56 * 2 ** 20
            ),
            cost_estimate=pl.CostEstimate(
                flops=units * 4 * tok * tok * DH,
                bytes_accessed=8 * query.size,
                transcendentals=units * tok * tok,
            ),
        )(pair_keys, pair_count, query, keys_in, values_in)

    tokens = P("ctx", "head", None)
    return jax.shard_map(
        body,
        mesh=mesh,
        in_specs=(tokens, tokens, tokens, P("ctx", None), P("ctx")),
        out_specs=tokens,
        check_vma=False,
    )
```

```python
import functools

import jax
import jax.numpy as jnp
from jax import lax
from jax.experimental import pallas as pl
from jax.experimental.pallas import tpu as pltpu
from jax.sharding import PartitionSpec as P

DH = 128
GROUP = 4
EXP2_SCALE = DH ** -0.5 * 1.4426950408889634
MASKED = 1e30
MESH = pl.DeviceIdType.MESH


def build_kernel(n_head, n_ctx, tiles, rows, heads, most):
    tok = n_head * rows

    def kernel(slots_ref, count_ref, q_ref, k_ref, v_ref, out_ref, *scratch):
        kwin, vwin = scratch[:heads], scratch[heads:2 * heads]
        q_all, v_all, o_all, rx, tx, win, wtx, o_rx, o_tx = scratch[2 * heads:]
        me_h, me_c = lax.axis_index("head"), lax.axis_index("ctx")
        first_slot = (me_c - 1) * tiles
        others = [lax.rem(me_h + step, n_head) for step in (1, n_head - 1, *range(2, n_head - 1))]

        barrier = pltpu.get_barrier_semaphore()
        for other in others:
            pl.semaphore_signal(barrier, inc=1, device_id={"head": other}, device_id_type=MESH)
        for other in (lax.rem(me_c + 1, n_ctx), lax.rem(me_c + n_ctx - 1, n_ctx)):
            pl.semaphore_signal(barrier, inc=1, device_id={"ctx": other}, device_id_type=MESH)
        pl.semaphore_wait(barrier, len(others) + 2)

        def head_columns(owner, g):
            return pl.ds(pl.multiple_of((owner * heads + g) * DH, DH), DH)

        def token_rows(owner):
            return pl.ds(pl.multiple_of(owner * rows, rows), rows)

        def landing(which, g):
            if which == 0:
                return kwin[g].at[tiles:2 * tiles]
            return (v_all if which == 1 else q_all).at[g]

        def send_inputs(g):
            for which, source in enumerate((k_ref, v_ref, q_ref)):
                target = landing(which, g).at[:, token_rows(me_h), :]
                for other in others:
                    pltpu.make_async_remote_copy(
                        src_ref=source.at[:, :, head_columns(other, g)],
                        dst_ref=target,
                        send_sem=tx.at[which],
                        recv_sem=rx.at[which, g],
                        device_id={"head": other},
                        device_id_type=MESH,
                    ).start()
                pltpu.make_async_copy(
                    source.at[:, :, head_columns(me_h, g)], target, rx.at[which, g]
                ).start()

        def await_bytes(ref, sem):
            pltpu.make_async_copy(ref, ref, sem).wait()

        def send_window(which, window, g, t):
            own = window[g].at[tiles + t]
            for side, (other, inside) in enumerate(((me_c + 1, me_c < n_ctx - 1), (me_c - 1, me_c > 0))):
                @pl.when(inside)
                def _():
                    pltpu.make_async_remote_copy(
                        src_ref=own,
                        dst_ref=window[g].at[2 * tiles * side + t],
                        send_sem=wtx.at[which, side, g],
                        recv_sem=win.at[which, g],
                        device_id={"ctx": other},
                        device_id_type=MESH,
                    ).start()

                @pl.when(jnp.logical_not(inside))
                def _():
                    pltpu.make_async_copy(
                        own, window[g].at[2 * tiles * (1 - side) + t], win.at[which, g]
                    ).start()

        def share_keys(g):
            await_bytes(landing(0, g), rx.at[0, g])

            def pass_on(t, carry):
                send_window(0, kwin, g, t)
                return carry

            lax.fori_loop(0, tiles, pass_on, 0)

        def share_values(g):
            await_bytes(landing(1, g), rx.at[1, g])

            def pass_on(t, carry):
                vwin[g][tiles + t] = v_all[g, t].T
                send_window(1, vwin, g, t)
                return carry

            lax.fori_loop(0, tiles, pass_on, 0)

        def compute(g):
            def one_tile(t, carry):
                query_t = q_all[g, t].T
                live = count_ref[t]
                top = jnp.full((1, tok), -MASKED, jnp.float32)
                total = jnp.zeros((1, tok), jnp.float32)
                out_t = jnp.zeros((DH, tok), jnp.float32)
                for base in range(0, most, GROUP):
                    scores, values, shifts = [], [], []
                    new_top = top
                    for p in range(base, base + GROUP):
                        slot = jnp.clip(slots_ref[t, p] - first_slot, 0, 3 * tiles - 1)
                        s = jnp.dot(kwin[g][slot], query_t, preferred_element_type=jnp.float32)
                        shift = jnp.where(p < live, 0.0, MASKED).astype(jnp.float32)
                        new_top = jnp.maximum(new_top, jnp.max(s, axis=0, keepdims=True) - shift)
                        scores.append(s)
                        values.append(vwin[g][slot])
                        shifts.append(shift)
                    top_scaled = new_top * EXP2_SCALE
                    old_factor = jnp.exp2(top * EXP2_SCALE - top_scaled)
                    total = total * old_factor
                    out_t = out_t * old_factor
                    for i in range(0, GROUP, 2):
                        weights = []
                        for s, shift in zip(scores[i:i + 2], shifts[i:i + 2]):
                            expo = jnp.exp2(s * EXP2_SCALE - (top_scaled + shift))
                            total = total + jnp.sum(expo, axis=0, keepdims=True)
                            weights.append(expo.astype(jnp.bfloat16))
                        out_t = out_t + jnp.dot(
                            jnp.concatenate(values[i:i + 2], axis=1),
                            jnp.concatenate(weights, axis=0),
                            preferred_element_type=jnp.float32,
                        )
                    top = new_top
                o_all[g, t] = (out_t / total).T.astype(jnp.bfloat16)
                send_output(g, t)
                for at, duty, ahead in ((0, share_keys, 1), (0, send_inputs, 3), (1, share_values, 1)):
                    if g + ahead < heads:
                        pl.when(t == at)(functools.partial(duty, g + ahead))
                return carry

            lax.fori_loop(0, tiles, one_tile, 0)

        def send_output(g, t):
            target = out_ref.at[t, :, head_columns(me_h, g)]
            for other in others:
                pltpu.make_async_remote_copy(
                    src_ref=o_all.at[g, t, token_rows(other), :],
                    dst_ref=target,
                    send_sem=o_tx.at[g],
                    recv_sem=o_rx.at[g],
                    device_id={"head": other},
                    device_id_type=MESH,
                ).start()
            pltpu.make_async_copy(
                o_all.at[g, t, token_rows(me_h), :], target, o_rx.at[g]
            ).start()

        for g in range(min(2, heads)):
            send_inputs(g)
        share_keys(0)
        share_values(0)
        if heads > 2:
            send_inputs(2)
        for g in range(heads):
            await_bytes(q_all.at[g], rx.at[2, g])
            await_bytes(kwin[g].at[:2 * tiles], win.at[0, g])
            await_bytes(vwin[g].at[:2 * tiles], win.at[1, g])
            compute(g)

        sent = tiles * (n_head - 1) // n_head
        for which, source in enumerate((k_ref, v_ref, q_ref)):
            await_bytes(source.at[:sent], tx.at[which])
        for g in range(heads):
            for which, window in enumerate((kwin, vwin)):
                for side, inside in enumerate((me_c < n_ctx - 1, me_c > 0)):
                    pl.when(inside)(
                        functools.partial(await_bytes, window[g].at[:tiles], wtx.at[which, side, g])
                    )
            await_bytes(o_all.at[g, :, :(n_head - 1) * rows, :], o_tx.at[g])
            await_bytes(o_all.at[g], o_rx.at[g])

    return kernel


def solution(mesh):
    n_head, n_ctx = mesh.shape["head"], mesh.shape["ctx"]

    def body(query, keys_in, values_in, pair_keys, pair_count):
        tiles, rows, width = query.shape
        most = pair_keys.shape[1]
        tok, heads = rows * n_head, width // DH // n_head
        units = tiles * most * heads
        dma = pltpu.SemaphoreType.DMA
        scratch = [pltpu.VMEM((3 * tiles, tok, DH), jnp.bfloat16)] * heads
        scratch += [pltpu.VMEM((3 * tiles, DH, tok), jnp.bfloat16)] * heads
        scratch += [pltpu.VMEM((heads, tiles, tok, DH), jnp.bfloat16)] * 3
        scratch += [dma((3, heads)), dma((3,)), dma((2, heads)), dma((2, 2, heads)), dma((heads,)), dma((heads,))]
        smem = pl.BlockSpec(memory_space=pltpu.SMEM)
        anywhere = pl.BlockSpec(memory_space=pl.ANY)
        return pl.pallas_call(
            build_kernel(n_head, n_ctx, tiles, rows, heads, most),
            out_shape=jax.ShapeDtypeStruct(query.shape, query.dtype),
            in_specs=[smem, smem, anywhere, anywhere, anywhere],
            out_specs=anywhere,
            scratch_shapes=scratch,
            compiler_params=pltpu.CompilerParams(
                collective_id=0, has_side_effects=True, vmem_limit_bytes=56 * 2 ** 20
            ),
            cost_estimate=pl.CostEstimate(
                flops=units * 4 * tok * tok * DH,
                bytes_accessed=8 * query.size,
                transcendentals=units * tok * tok,
            ),
        )(pair_keys, pair_count, query, keys_in, values_in)

    tokens = P("ctx", "head", None)
    return jax.shard_map(
        body,
        mesh=mesh,
        in_specs=(tokens, tokens, tokens, P("ctx", None), P("ctx")),
        out_specs=tokens,
        check_vma=False,
    )
```

```python
import functools

import jax
import jax.numpy as jnp
from jax import lax
from jax.experimental import pallas as pl
from jax.experimental.pallas import tpu as pltpu
from jax.sharding import PartitionSpec as P

DH = 128
EXP2_SCALE = DH ** -0.5 * 1.4426950408889634
MASKED = 1e30
MESH = pl.DeviceIdType.MESH


def build_kernel(n_head, n_ctx, tiles, rows, heads, most):
    tok = n_head * rows

    def kernel(slots_ref, count_ref, q_ref, k_ref, v_ref, out_ref, *scratch):
        kwin, vwin = scratch[:heads], scratch[heads:2 * heads]
        q_all, k_all, o_all, rx, tx, win, wtx, o_rx, o_tx = scratch[2 * heads:]
        me_h, me_c = lax.axis_index("head"), lax.axis_index("ctx")
        first_slot = (me_c - 1) * tiles
        others = [lax.rem(me_h + step, n_head) for step in (1, n_head - 1, *range(2, n_head - 1))]

        barrier = pltpu.get_barrier_semaphore()
        for other in others:
            pl.semaphore_signal(barrier, inc=1, device_id={"head": other}, device_id_type=MESH)
        ctx_sides = ((me_c + 1, me_c < n_ctx - 1), (me_c - 1, me_c > 0))
        for other, inside in ctx_sides:
            @pl.when(inside)
            def _():
                pl.semaphore_signal(barrier, inc=1, device_id={"ctx": other}, device_id_type=MESH)
        at_edge = jnp.logical_or(me_c == 0, me_c == n_ctx - 1)
        for edge, partners in ((at_edge, len(others) + 1), (jnp.logical_not(at_edge), len(others) + 2)):
            pl.when(edge)(functools.partial(pl.semaphore_wait, barrier, partners))

        def head_columns(owner, g):
            return pl.ds(pl.multiple_of((owner * heads + g) * DH, DH), DH)

        def token_rows(owner):
            return pl.ds(pl.multiple_of(owner * rows, rows), rows)

        def landing(which, g):
            if which == 1:
                return vwin[g].at[tiles:2 * tiles]
            return (k_all if which == 0 else q_all).at[g]

        def send_inputs(kinds, g):
            for which in kinds:
                source = (k_ref, v_ref, q_ref)[which]
                target = landing(which, g).at[:, token_rows(me_h), :]
                for other in others:
                    pltpu.make_async_remote_copy(
                        src_ref=source.at[:, :, head_columns(other, g)],
                        dst_ref=target,
                        send_sem=tx.at[which],
                        recv_sem=rx.at[which, g],
                        device_id={"head": other},
                        device_id_type=MESH,
                    ).start()
                pltpu.make_async_copy(
                    source.at[:, :, head_columns(me_h, g)], target, rx.at[which, g]
                ).start()

        def await_bytes(ref, sem):
            pltpu.make_async_copy(ref, ref, sem).wait()

        def send_window(which, window, g, t):
            own = window[g].at[tiles + t]
            for side, (other, inside) in enumerate(ctx_sides):
                @pl.when(inside)
                def _():
                    pltpu.make_async_remote_copy(
                        src_ref=own,
                        dst_ref=window[g].at[2 * tiles * side + t],
                        send_sem=wtx.at[which, side, g],
                        recv_sem=win.at[which, g],
                        device_id={"ctx": other},
                        device_id_type=MESH,
                    ).start()

                @pl.when(jnp.logical_not(inside))
                def _():
                    pltpu.make_async_copy(
                        own, window[g].at[2 * tiles * (1 - side) + t], win.at[which, g]
                    ).start()

        def share_keys(g):
            await_bytes(landing(0, g), rx.at[0, g])

            def pass_on(t, carry):
                kwin[g][tiles + t] = k_all[g, t].T
                send_window(0, kwin, g, t)
                return carry

            lax.fori_loop(0, tiles, pass_on, 0)

        def share_values(g):
            await_bytes(landing(1, g), rx.at[1, g])

            def pass_on(t, carry):
                send_window(1, vwin, g, t)
                return carry

            lax.fori_loop(0, tiles, pass_on, 0)

        def compute(g, duties):
            def one_tile(t, carry):
                query = q_all[g, t]
                live = count_ref[t]
                shifts = [jnp.where(p < live, 0.0, MASKED).astype(jnp.float32) for p in range(most)]
                slots = [jnp.clip(slots_ref[t, p] - first_slot, 0, 3 * tiles - 1) for p in range(most)]
                scores, top = [], jnp.full((tok, DH), -MASKED, jnp.float32)
                for p in range(0, most, 2):
                    keys = jnp.concatenate([kwin[g][slots[p]], kwin[g][slots[p + 1]]], axis=1)
                    both = jnp.dot(query, keys, preferred_element_type=jnp.float32)
                    for s, shift in zip((both[:, :tok], both[:, tok:]), shifts[p:p + 2]):
                        most_of = s[:, :DH]
                        for at in range(DH, tok, DH):
                            most_of = jnp.maximum(most_of, s[:, at:at + DH])
                        top = jnp.maximum(top, most_of - shift)
                        scores.append(s)
                top = jnp.max(top, axis=1, keepdims=True) * EXP2_SCALE
                ones = jnp.ones((2 * tok, DH), jnp.bfloat16)
                merged = jnp.zeros((tok, 2 * DH), jnp.float32)
                for p in range(0, most, 2):
                    weights = [
                        jnp.exp2(s * EXP2_SCALE - (top + shift)).astype(jnp.bfloat16)
                        for s, shift in zip(scores[p:p + 2], shifts[p:p + 2])
                    ]
                    values = jnp.concatenate([vwin[g][slots[p]], vwin[g][slots[p + 1]]], axis=0)
                    merged = merged + jnp.dot(
                        jnp.concatenate(weights, axis=1),
                        jnp.concatenate([values, ones], axis=1),
                        preferred_element_type=jnp.float32,
                    )
                o_all[g, t] = (merged[:, :DH] / merged[:, DH:]).astype(jnp.bfloat16)
                if g == heads - 1:
                    send_output(g, t)
                for at, duty in duties:
                    pl.when(t == at)(duty)
                return carry

            lax.fori_loop(0, tiles, one_tile, 0)

        def send_output(g, t):
            target = out_ref.at[t, :, head_columns(me_h, g)]
            for other in others:
                pltpu.make_async_remote_copy(
                    src_ref=o_all.at[g, t, token_rows(other), :],
                    dst_ref=target,
                    send_sem=o_tx.at[g],
                    recv_sem=o_rx.at[g],
                    device_id={"head": other},
                    device_id_type=MESH,
                ).start()
            pltpu.make_async_copy(
                o_all.at[g, t, token_rows(me_h), :], target, o_rx.at[g]
            ).start()

        def send_outputs(g):
            def one_tile(t, carry):
                send_output(g, t)
                return carry

            lax.fori_loop(0, tiles, one_tile, 0)

        def later(duty, *args):
            return functools.partial(duty, *args) if args[-1] < heads else lambda: None

        send_inputs((0, 1, 2), 0)
        later(send_inputs, (0, 1), 1)()
        share_keys(0)
        share_values(0)
        later(send_inputs, (2,), 1)()
        later(send_inputs, (0, 1), 2)()
        for g in range(heads):
            duties = [(0, later(send_inputs, (0, 1), g + 3)), (0, later(send_inputs, (2,), g + 2))]
            sharing = [(0, later(share_keys, g + 1)), (1, later(share_values, g + 1))]
            if g < heads // 2:
                duties = sharing + duties
            else:
                for _, duty in sharing:
                    duty()
            if g == heads - 2:
                duties += [(min(held, tiles - 1), later(send_outputs, held)) for held in range(g)]
            elif g == heads - 1 and g > 0:
                duties.append((0, later(send_outputs, g - 1)))
            await_bytes(q_all.at[g], rx.at[2, g])
            await_bytes(kwin[g].at[:2 * tiles], win.at[0, g])
            await_bytes(vwin[g].at[:2 * tiles], win.at[1, g])
            compute(g, duties)

        sent = tiles * (n_head - 1) // n_head
        for which, source in enumerate((k_ref, v_ref, q_ref)):
            await_bytes(source.at[:sent], tx.at[which])
        for g in range(heads):
            for which, window in enumerate((kwin, vwin)):
                for side, (_, inside) in enumerate(ctx_sides):
                    pl.when(inside)(
                        functools.partial(await_bytes, window[g].at[:tiles], wtx.at[which, side, g])
                    )
            await_bytes(o_all.at[g, :, :(n_head - 1) * rows, :], o_tx.at[g])
            await_bytes(o_all.at[g], o_rx.at[g])

    return kernel


def solution(mesh):
    n_head, n_ctx = mesh.shape["head"], mesh.shape["ctx"]

    def body(query, keys_in, values_in, pair_keys, pair_count):
        tiles, rows, width = query.shape
        most = pair_keys.shape[1]
        tok, heads = rows * n_head, width // DH // n_head
        units = tiles * most * heads
        dma = pltpu.SemaphoreType.DMA
        scratch = [pltpu.VMEM((3 * tiles, DH, tok), jnp.bfloat16)] * heads
        scratch += [pltpu.VMEM((3 * tiles, tok, DH), jnp.bfloat16)] * heads
        scratch += [pltpu.VMEM((heads, tiles, tok, DH), jnp.bfloat16)] * 3
        scratch += [dma((3, heads)), dma((3,)), dma((2, heads)), dma((2, 2, heads)), dma((heads,)), dma((heads,))]
        smem = pl.BlockSpec(memory_space=pltpu.SMEM)
        anywhere = pl.BlockSpec(memory_space=pl.ANY)
        return pl.pallas_call(
            build_kernel(n_head, n_ctx, tiles, rows, heads, most),
            out_shape=jax.ShapeDtypeStruct(query.shape, query.dtype),
            in_specs=[smem, smem, anywhere, anywhere, anywhere],
            out_specs=anywhere,
            scratch_shapes=scratch,
            compiler_params=pltpu.CompilerParams(
                collective_id=0, has_side_effects=True, vmem_limit_bytes=56 * 2 ** 20
            ),
            cost_estimate=pl.CostEstimate(
                flops=units * 4 * tok * tok * DH,
                bytes_accessed=8 * query.size,
                transcendentals=units * tok * tok,
            ),
        )(pair_keys, pair_count, query, keys_in, values_in)

    tokens = P("ctx", "head", None)
    return jax.shard_map(
        body,
        mesh=mesh,
        in_specs=(tokens, tokens, tokens, P("ctx", None), P("ctx")),
        out_specs=tokens,
        check_vma=False,
    )
```

```python
import functools

import jax
import jax.numpy as jnp
from jax import lax
from jax.experimental import pallas as pl
from jax.experimental.pallas import tpu as pltpu
from jax.sharding import PartitionSpec as P

DH = 128
EXP2_SCALE = DH ** -0.5 * 1.4426950408889634
MASKED = 1e30
MESH = pl.DeviceIdType.MESH


def build_kernel(n_head, n_ctx, tiles, rows, heads, most):
    tok = n_head * rows

    def kernel(slots_ref, count_ref, q_ref, k_ref, v_ref, out_ref, *scratch):
        kwin, vwin = scratch[:heads], scratch[heads:2 * heads]
        q_all, k_all, o_all, *rest = scratch[2 * heads:]
        score_bufs, tops = rest[:2], rest[2:4]
        rx, tx, win, wtx, o_rx, o_tx = rest[4:]
        me_h, me_c = lax.axis_index("head"), lax.axis_index("ctx")
        first_slot = (me_c - 1) * tiles
        others = [lax.rem(me_h + step, n_head) for step in (1, n_head - 1, *range(2, n_head - 1))]

        barrier = pltpu.get_barrier_semaphore()
        for other in others:
            pl.semaphore_signal(barrier, inc=1, device_id={"head": other}, device_id_type=MESH)
        ctx_sides = ((me_c + 1, me_c < n_ctx - 1), (me_c - 1, me_c > 0))
        for other, inside in ctx_sides:
            @pl.when(inside)
            def _():
                pl.semaphore_signal(barrier, inc=1, device_id={"ctx": other}, device_id_type=MESH)
        at_edge = jnp.logical_or(me_c == 0, me_c == n_ctx - 1)
        for edge, partners in ((at_edge, len(others) + 1), (jnp.logical_not(at_edge), len(others) + 2)):
            pl.when(edge)(functools.partial(pl.semaphore_wait, barrier, partners))

        def head_columns(owner, g):
            return pl.ds(pl.multiple_of((owner * heads + g) * DH, DH), DH)

        def token_rows(owner):
            return pl.ds(pl.multiple_of(owner * rows, rows), rows)

        def landing(which, g):
            if which == 1:
                return vwin[g].at[tiles:2 * tiles]
            return (k_all if which == 0 else q_all).at[g]

        def send_inputs(kinds, g):
            for which in kinds:
                source = (k_ref, v_ref, q_ref)[which]
                target = landing(which, g).at[:, token_rows(me_h), :]
                for other in others:
                    pltpu.make_async_remote_copy(
                        src_ref=source.at[:, :, head_columns(other, g)],
                        dst_ref=target,
                        send_sem=tx.at[which],
                        recv_sem=rx.at[which, g],
                        device_id={"head": other},
                        device_id_type=MESH,
                    ).start()
                pltpu.make_async_copy(
                    source.at[:, :, head_columns(me_h, g)], target, rx.at[which, g]
                ).start()

        def await_bytes(ref, sem):
            pltpu.make_async_copy(ref, ref, sem).wait()

        def send_window(which, window, g, t):
            own = window[g].at[tiles + t]
            for side, (other, inside) in enumerate(ctx_sides):
                @pl.when(inside)
                def _():
                    pltpu.make_async_remote_copy(
                        src_ref=own,
                        dst_ref=window[g].at[2 * tiles * side + t],
                        send_sem=wtx.at[which, side, g],
                        recv_sem=win.at[which, g],
                        device_id={"ctx": other},
                        device_id_type=MESH,
                    ).start()

                @pl.when(jnp.logical_not(inside))
                def _():
                    pltpu.make_async_copy(
                        own, window[g].at[2 * tiles * (1 - side) + t], win.at[which, g]
                    ).start()

        def share_keys(g):
            await_bytes(landing(0, g), rx.at[0, g])

            def pass_on(t, carry):
                kwin[g][tiles + t] = k_all[g, t].T
                send_window(0, kwin, g, t)
                return carry

            lax.fori_loop(0, tiles, pass_on, 0)

        def share_values(g):
            await_bytes(landing(1, g), rx.at[1, g])

            def pass_on(t, carry):
                send_window(1, vwin, g, t)
                return carry

            lax.fori_loop(0, tiles, pass_on, 0)

        half = tok // 2

        def pair_of(t, p):
            slot = jnp.clip(slots_ref[t, p] - first_slot, 0, 3 * tiles - 1)
            return slot, jnp.where(p < count_ref[t], 0.0, MASKED).astype(jnp.float32)

        def half_step(g, done, coming):
            if coming is not None:
                t_in, side_in = coming
                query = q_all[g, t_in, side_in * half:(side_in + 1) * half]
                top_in = jnp.full((half, DH), -MASKED, jnp.float32)
            if done is not None:
                t_out, side_out = done
                top_out = tops[side_out][...]
                merged = jnp.zeros((half, 2 * DH), jnp.float32)
                ones = jnp.ones((2 * tok, DH), jnp.bfloat16)
            for p in range(0, most, 2):
                if coming is not None:
                    (slot0, shift0), (slot1, shift1) = pair_of(t_in, p), pair_of(t_in, p + 1)
                    keys = jnp.concatenate([kwin[g][slot0], kwin[g][slot1]], axis=1)
                    both = jnp.dot(query, keys, preferred_element_type=jnp.float32)
                    score_bufs[side_in][:, p * tok:(p + 2) * tok] = both
                    for start, shift in ((0, shift0), (tok, shift1)):
                        most_of = both[:, start:start + DH]
                        for at in range(start + DH, start + tok, DH):
                            most_of = jnp.maximum(most_of, both[:, at:at + DH])
                        top_in = jnp.maximum(top_in, most_of - shift)
                if done is not None:
                    (slot0, shift0), (slot1, shift1) = pair_of(t_out, p), pair_of(t_out, p + 1)
                    weights = []
                    for start, shift in ((p * tok, shift0), ((p + 1) * tok, shift1)):
                        base = top_out + shift
                        for at in range(start, start + tok, DH):
                            s = score_bufs[side_out][:, at:at + DH]
                            weights.append(jnp.exp2(s * EXP2_SCALE - base).astype(jnp.bfloat16))
                    values = jnp.concatenate([vwin[g][slot0], vwin[g][slot1]], axis=0)
                    merged = merged + jnp.dot(
                        jnp.concatenate(weights, axis=1),
                        jnp.concatenate([values, ones], axis=1),
                        preferred_element_type=jnp.float32,
                    )
            if coming is not None:
                top_in = jnp.max(top_in, axis=1, keepdims=True) * EXP2_SCALE
                tops[side_in][...] = jnp.broadcast_to(top_in, (half, DH))
            if done is not None:
                o_all[g, t_out, side_out * half:(side_out + 1) * half] = (
                    merged[:, :DH] / merged[:, DH:]
                ).astype(jnp.bfloat16)

        def compute(g, duties):
            def one_tile(t, carry):
                half_step(g, (t, 0), (t, 1))
                half_step(g, (t, 1), (jnp.minimum(t + 1, tiles - 1), 0))
                if g == heads - 1:
                    send_output(g, t)
                for at, duty in duties:
                    pl.when(t == at)(duty)
                return carry

            half_step(g, None, (0, 0))
            lax.fori_loop(0, tiles, one_tile, 0)

        def send_output(g, t):
            target = out_ref.at[t, :, head_columns(me_h, g)]
            for other in others:
                pltpu.make_async_remote_copy(
                    src_ref=o_all.at[g, t, token_rows(other), :],
                    dst_ref=target,
                    send_sem=o_tx.at[g],
                    recv_sem=o_rx.at[g],
                    device_id={"head": other},
                    device_id_type=MESH,
                ).start()
            pltpu.make_async_copy(
                o_all.at[g, t, token_rows(me_h), :], target, o_rx.at[g]
            ).start()

        def send_outputs(g):
            def one_tile(t, carry):
                send_output(g, t)
                return carry

            lax.fori_loop(0, tiles, one_tile, 0)

        def later(duty, *args):
            return functools.partial(duty, *args) if args[-1] < heads else lambda: None

        send_inputs((0, 1, 2), 0)
        later(send_inputs, (0, 1), 1)()
        share_keys(0)
        share_values(0)
        later(send_inputs, (2,), 1)()
        later(send_inputs, (0, 1), 2)()
        for g in range(heads):
            duties = [(0, later(send_inputs, (0, 1), g + 3)), (0, later(send_inputs, (2,), g + 2))]
            sharing = [(0, later(share_keys, g + 1)), (1, later(share_values, g + 1))]
            if g < heads // 2:
                duties = sharing + duties
            else:
                for _, duty in sharing:
                    duty()
            if g == heads - 2:
                duties += [(min(held, tiles - 1), later(send_outputs, held)) for held in range(g)]
            elif g == heads - 1 and g > 0:
                duties.append((0, later(send_outputs, g - 1)))
            await_bytes(q_all.at[g], rx.at[2, g])
            await_bytes(kwin[g].at[:2 * tiles], win.at[0, g])
            await_bytes(vwin[g].at[:2 * tiles], win.at[1, g])
            compute(g, duties)

        sent = tiles * (n_head - 1) // n_head
        for which, source in enumerate((k_ref, v_ref, q_ref)):
            await_bytes(source.at[:sent], tx.at[which])
        for g in range(heads):
            for which, window in enumerate((kwin, vwin)):
                for side, (_, inside) in enumerate(ctx_sides):
                    pl.when(inside)(
                        functools.partial(await_bytes, window[g].at[:tiles], wtx.at[which, side, g])
                    )
            await_bytes(o_all.at[g, :, :(n_head - 1) * rows, :], o_tx.at[g])
            await_bytes(o_all.at[g], o_rx.at[g])

    return kernel


def solution(mesh):
    n_head, n_ctx = mesh.shape["head"], mesh.shape["ctx"]

    def body(query, keys_in, values_in, pair_keys, pair_count):
        tiles, rows, width = query.shape
        most = pair_keys.shape[1]
        tok, heads = rows * n_head, width // DH // n_head
        units = tiles * most * heads
        dma = pltpu.SemaphoreType.DMA
        scratch = [pltpu.VMEM((3 * tiles, DH, tok), jnp.bfloat16)] * heads
        scratch += [pltpu.VMEM((3 * tiles, tok, DH), jnp.bfloat16)] * heads
        scratch += [pltpu.VMEM((heads, tiles, tok, DH), jnp.bfloat16)] * 3
        scratch += [pltpu.VMEM((tok // 2, most * tok), jnp.float32)] * 2
        scratch += [pltpu.VMEM((tok // 2, DH), jnp.float32)] * 2
        scratch += [dma((3, heads)), dma((3,)), dma((2, heads)), dma((2, 2, heads)), dma((heads,)), dma((heads,))]
        smem = pl.BlockSpec(memory_space=pltpu.SMEM)
        in_hbm = pl.BlockSpec(memory_space=pltpu.HBM)
        return pl.pallas_call(
            build_kernel(n_head, n_ctx, tiles, rows, heads, most),
            out_shape=pltpu.VMEM(query.shape, query.dtype),
            in_specs=[smem, smem, in_hbm, in_hbm, in_hbm],
            out_specs=pl.BlockSpec(memory_space=pltpu.VMEM),
            scratch_shapes=scratch,
            compiler_params=pltpu.CompilerParams(
                collective_id=0, has_side_effects=True, vmem_limit_bytes=60 * 2 ** 20
            ),
            cost_estimate=pl.CostEstimate(
                flops=units * 4 * tok * tok * DH,
                bytes_accessed=8 * query.size,
                transcendentals=units * tok * tok,
            ),
        )(pair_keys, pair_count, query, keys_in, values_in)

    tokens = P("ctx", "head", None)
    return jax.shard_map(
        body,
        mesh=mesh,
        in_specs=(tokens, tokens, tokens, P("ctx", None), P("ctx")),
        out_specs=tokens,
        check_vma=False,
    )
```

```python
import functools

import jax
import jax.numpy as jnp
from jax import lax
from jax.experimental import pallas as pl
from jax.experimental.pallas import tpu as pltpu
from jax.sharding import PartitionSpec as P

DH = 128
EXP2_SCALE = DH ** -0.5 * 1.4426950408889634
MASKED = 1e30
MESH = pl.DeviceIdType.MESH


def build_kernel(n_head, n_ctx, tiles, rows, heads, most):
    tok = n_head * rows

    def kernel(slots_hbm, count_hbm, q_ref, k_ref, v_ref, out_ref, *scratch):
        kwin, vwin = scratch[:heads], scratch[heads:2 * heads]
        q_all, k_all, o_all, *rest = scratch[2 * heads:]
        score_bufs, tops = rest[:2], rest[2:4]
        slots_ref, count_ref = rest[4:6]
        rx, tx, win, wtx, o_rx, o_tx, lists = rest[6:]
        me_h, me_c = lax.axis_index("head"), lax.axis_index("ctx")
        first_slot = (me_c - 1) * tiles
        others = [lax.rem(me_h + step, n_head) for step in (1, n_head - 1, *range(2, n_head - 1))]

        barrier = pltpu.get_barrier_semaphore()
        for other in others:
            pl.semaphore_signal(barrier, inc=1, device_id={"head": other}, device_id_type=MESH)
        ctx_sides = ((me_c + 1, me_c < n_ctx - 1), (me_c - 1, me_c > 0))
        for other, inside in ctx_sides:
            @pl.when(inside)
            def _():
                pl.semaphore_signal(barrier, inc=1, device_id={"ctx": other}, device_id_type=MESH)
        at_edge = jnp.logical_or(me_c == 0, me_c == n_ctx - 1)
        for edge, partners in ((at_edge, len(others) + 1), (jnp.logical_not(at_edge), len(others) + 2)):
            pl.when(edge)(functools.partial(pl.semaphore_wait, barrier, partners))

        def head_columns(owner, g):
            return pl.ds(pl.multiple_of((owner * heads + g) * DH, DH), DH)

        def token_rows(owner):
            return pl.ds(pl.multiple_of(owner * rows, rows), rows)

        def landing(which, g):
            if which == 1:
                return vwin[g].at[tiles:2 * tiles]
            return (k_all if which == 0 else q_all).at[g]

        def send_inputs(kinds, g):
            for which in kinds:
                source = (k_ref, v_ref, q_ref)[which]
                target = landing(which, g).at[:, token_rows(me_h), :]
                for other in others:
                    pltpu.make_async_remote_copy(
                        src_ref=source.at[:, :, head_columns(other, g)],
                        dst_ref=target,
                        send_sem=tx.at[which],
                        recv_sem=rx.at[which, g],
                        device_id={"head": other},
                        device_id_type=MESH,
                    ).start()
            for which in kinds:
                pltpu.make_async_copy(
                    (k_ref, v_ref, q_ref)[which].at[:, :, head_columns(me_h, g)],
                    landing(which, g).at[:, token_rows(me_h), :],
                    rx.at[which, g],
                ).start()

        def await_bytes(ref, sem):
            pltpu.make_async_copy(ref, ref, sem).wait()

        def send_window(which, window, g, t):
            own = window[g].at[tiles + t]
            for side, (other, inside) in enumerate(ctx_sides):
                @pl.when(inside)
                def _():
                    pltpu.make_async_remote_copy(
                        src_ref=own,
                        dst_ref=window[g].at[2 * tiles * side + t],
                        send_sem=wtx.at[which, side, g],
                        recv_sem=win.at[which, g],
                        device_id={"ctx": other},
                        device_id_type=MESH,
                    ).start()

                @pl.when(jnp.logical_not(inside))
                def _():
                    pltpu.make_async_copy(
                        own, window[g].at[2 * tiles * (1 - side) + t], win.at[which, g]
                    ).start()

        def share_keys(g):
            await_bytes(landing(0, g), rx.at[0, g])

            def pass_on(t, carry):
                kwin[g][tiles + t] = k_all[g, t].T
                send_window(0, kwin, g, t)
                return carry

            lax.fori_loop(0, tiles, pass_on, 0)

        def share_values(g):
            await_bytes(landing(1, g), rx.at[1, g])

            def pass_on(t, carry):
                send_window(1, vwin, g, t)
                return carry

            lax.fori_loop(0, tiles, pass_on, 0)

        half = tok // 2

        def pair_of(t, p):
            slot = jnp.clip(slots_ref[t, p] - first_slot, 0, 3 * tiles - 1)
            return slot, jnp.where(p < count_ref[t], 0.0, MASKED).astype(jnp.float32)

        def half_step(g, done, coming):
            if coming is not None:
                t_in, side_in = coming
                query = q_all[g, t_in, side_in * half:(side_in + 1) * half]
                top_in = jnp.full((half, DH), -MASKED, jnp.float32)
            if done is not None:
                t_out, side_out = done
                top_out = tops[side_out][...]
                merged = jnp.zeros((half, 2 * DH), jnp.float32)
                ones = jnp.ones((2 * tok, DH), jnp.bfloat16)
            for p in range(0, most, 2):
                if coming is not None:
                    (slot0, shift0), (slot1, shift1) = pair_of(t_in, p), pair_of(t_in, p + 1)
                    keys = jnp.concatenate([kwin[g][slot0], kwin[g][slot1]], axis=1)
                    both = jnp.dot(query, keys, preferred_element_type=jnp.float32)
                    score_bufs[side_in][:, p * tok:(p + 2) * tok] = both
                    for start, shift in ((0, shift0), (tok, shift1)):
                        most_of = both[:, start:start + DH]
                        for at in range(start + DH, start + tok, DH):
                            most_of = jnp.maximum(most_of, both[:, at:at + DH])
                        top_in = jnp.maximum(top_in, most_of - shift)
                if done is not None:
                    (slot0, shift0), (slot1, shift1) = pair_of(t_out, p), pair_of(t_out, p + 1)
                    weights = []
                    for start, shift in ((p * tok, shift0), ((p + 1) * tok, shift1)):
                        base = top_out + shift
                        for at in range(start, start + tok, DH):
                            s = score_bufs[side_out][:, at:at + DH]
                            weights.append(jnp.exp2(s * EXP2_SCALE - base).astype(jnp.bfloat16))
                    values = jnp.concatenate([vwin[g][slot0], vwin[g][slot1]], axis=0)
                    merged = merged + jnp.dot(
                        jnp.concatenate(weights, axis=1),
                        jnp.concatenate([values, ones], axis=1),
                        preferred_element_type=jnp.float32,
                    )
            if coming is not None:
                top_in = jnp.max(top_in, axis=1, keepdims=True) * EXP2_SCALE
                tops[side_in][...] = jnp.broadcast_to(top_in, (half, DH))
            if done is not None:
                o_all[g, t_out, side_out * half:(side_out + 1) * half] = (
                    merged[:, :DH] / merged[:, DH:]
                ).astype(jnp.bfloat16)

        def compute(g, duties):
            def one_tile(t, carry):
                half_step(g, (t, 0), (t, 1))
                half_step(g, (t, 1), (jnp.minimum(t + 1, tiles - 1), 0))
                if g == heads - 1:
                    send_output(g, t)
                for at, duty in duties:
                    pl.when(t == at)(duty)
                return carry

            half_step(g, None, (0, 0))
            lax.fori_loop(0, tiles, one_tile, 0)

        def send_output(g, ts):
            target = out_ref.at[ts, :, head_columns(me_h, g)]
            for other in others:
                pltpu.make_async_remote_copy(
                    src_ref=o_all.at[g, ts, token_rows(other), :],
                    dst_ref=target,
                    send_sem=o_tx.at[g],
                    recv_sem=o_rx.at[g],
                    device_id={"head": other},
                    device_id_type=MESH,
                ).start()
            pltpu.make_async_copy(
                o_all.at[g, ts, token_rows(me_h), :], target, o_rx.at[g]
            ).start()

        def send_outputs(g):
            send_output(g, slice(None))

        def later(duty, *args):
            return functools.partial(duty, *args) if args[-1] < heads else lambda: None

        send_inputs((0, 1, 2), 0)
        later(send_inputs, (0, 1), 1)()
        list_copies = [
            pltpu.make_async_copy(source, target, lists.at[i])
            for i, (source, target) in enumerate(((slots_hbm, slots_ref), (count_hbm, count_ref)))
        ]
        for copy in list_copies:
            copy.start()
        share_keys(0)
        share_values(0)
        later(send_inputs, (2,), 1)()
        later(send_inputs, (0, 1), 2)()
        for copy in list_copies:
            copy.wait()
        for g in range(heads):
            duties = [(0, later(send_inputs, (0, 1), g + 3)), (0, later(send_inputs, (2,), g + 2))]
            sharing = [(0, later(share_keys, g + 1)), (1, later(share_values, g + 1))]
            if g < heads // 2:
                duties = sharing + duties
            else:
                for _, duty in sharing:
                    duty()
            if g == heads - 2:
                duties += [(min(held, tiles - 1), later(send_outputs, held)) for held in range(g)]
            elif g == heads - 1 and g > 0:
                duties.append((0, later(send_outputs, g - 1)))
            await_bytes(q_all.at[g], rx.at[2, g])
            await_bytes(kwin[g].at[:2 * tiles], win.at[0, g])
            await_bytes(vwin[g].at[:2 * tiles], win.at[1, g])
            compute(g, duties)

        sent = tiles * (n_head - 1) // n_head
        for which, source in enumerate((k_ref, v_ref, q_ref)):
            await_bytes(source.at[:sent], tx.at[which])
        for g in range(heads):
            for which, window in enumerate((kwin, vwin)):
                for side, (_, inside) in enumerate(ctx_sides):
                    pl.when(inside)(
                        functools.partial(await_bytes, window[g].at[:tiles], wtx.at[which, side, g])
                    )
            await_bytes(o_all.at[g, :, :(n_head - 1) * rows, :], o_tx.at[g])
            await_bytes(o_all.at[g], o_rx.at[g])

    return kernel


def solution(mesh):
    n_head, n_ctx = mesh.shape["head"], mesh.shape["ctx"]

    def body(query, keys_in, values_in, pair_keys, pair_count):
        tiles, rows, width = query.shape
        most = pair_keys.shape[1]
        tok, heads = rows * n_head, width // DH // n_head
        units = tiles * most * heads
        dma = pltpu.SemaphoreType.DMA
        scratch = [pltpu.VMEM((3 * tiles, DH, tok), jnp.bfloat16)] * heads
        scratch += [pltpu.VMEM((3 * tiles, tok, DH), jnp.bfloat16)] * heads
        scratch += [pltpu.VMEM((heads, tiles, tok, DH), jnp.bfloat16)] * 3
        scratch += [pltpu.VMEM((tok // 2, most * tok), jnp.float32)] * 2
        scratch += [pltpu.VMEM((tok // 2, DH), jnp.float32)] * 2
        scratch += [pltpu.SMEM(pair_keys.shape, jnp.int32), pltpu.SMEM(pair_count.shape, jnp.int32)]
        scratch += [dma((3, heads)), dma((3,)), dma((2, heads)), dma((2, 2, heads)), dma((heads,)), dma((heads,)), dma((2,))]
        in_hbm = pl.BlockSpec(memory_space=pltpu.HBM)
        return pl.pallas_call(
            build_kernel(n_head, n_ctx, tiles, rows, heads, most),
            out_shape=pltpu.VMEM(query.shape, query.dtype),
            in_specs=[in_hbm] * 5,
            out_specs=pl.BlockSpec(memory_space=pltpu.VMEM),
            scratch_shapes=scratch,
            compiler_params=pltpu.CompilerParams(
                collective_id=0, has_side_effects=True, vmem_limit_bytes=60 * 2 ** 20
            ),
            cost_estimate=pl.CostEstimate(
                flops=units * 4 * tok * tok * DH,
                bytes_accessed=8 * query.size,
                transcendentals=units * tok * tok,
            ),
        )(pair_keys, pair_count, query, keys_in, values_in)

    tokens = P("ctx", "head", None)
    return jax.shard_map(
        body,
        mesh=mesh,
        in_specs=(tokens, tokens, tokens, P("ctx", None), P("ctx")),
        out_specs=tokens,
        check_vma=False,
    )
```

```python
import functools

import jax
import jax.numpy as jnp
from jax import lax
from jax.experimental import pallas as pl
from jax.experimental.pallas import tpu as pltpu
from jax.sharding import PartitionSpec as P

DH = 128
EXP2_SCALE = DH ** -0.5 * 1.4426950408889634
MASKED = 1e30
MESH = pl.DeviceIdType.MESH


def build_kernel(n_head, n_ctx, tiles, rows, heads, most):
    tok = n_head * rows

    def kernel(slots_hbm, count_hbm, q_ref, k_ref, v_ref, out_ref, *scratch):
        kwin, vwin = scratch[:heads], scratch[heads:2 * heads]
        q_all, k_all, o_all, *rest = scratch[2 * heads:]
        score_bufs, tops = rest[:2], rest[2:4]
        slots_ref, count_ref = rest[4:6]
        rx, tx, win, wtx, o_rx, o_tx, lists = rest[6:]
        me_h, me_c = lax.axis_index("head"), lax.axis_index("ctx")
        first_slot = (me_c - 1) * tiles
        others = [lax.rem(me_h + step, n_head) for step in (1, n_head - 1, *range(2, n_head - 1))]

        barrier = pltpu.get_barrier_semaphore()
        for other in others:
            pl.semaphore_signal(barrier, inc=1, device_id={"head": other}, device_id_type=MESH)
        ctx_sides = ((me_c + 1, me_c < n_ctx - 1), (me_c - 1, me_c > 0))
        for other, inside in ctx_sides:
            @pl.when(inside)
            def _():
                pl.semaphore_signal(barrier, inc=1, device_id={"ctx": other}, device_id_type=MESH)
        at_edge = jnp.logical_or(me_c == 0, me_c == n_ctx - 1)
        for edge, partners in ((at_edge, len(others) + 1), (jnp.logical_not(at_edge), len(others) + 2)):
            pl.when(edge)(functools.partial(pl.semaphore_wait, barrier, partners))

        def head_columns(owner, g):
            return pl.ds(pl.multiple_of((owner * heads + g) * DH, DH), DH)

        def token_rows(owner):
            return pl.ds(pl.multiple_of(owner * rows, rows), rows)

        def landing(which, g):
            if which == 1:
                return vwin[g].at[tiles:2 * tiles]
            return (k_all if which == 0 else q_all).at[g]

        def send_inputs(kinds, g):
            for which in kinds:
                source = (k_ref, v_ref, q_ref)[which]
                target = landing(which, g).at[:, token_rows(me_h), :]
                for other in others:
                    pltpu.make_async_remote_copy(
                        src_ref=source.at[:, :, head_columns(other, g)],
                        dst_ref=target,
                        send_sem=tx.at[which],
                        recv_sem=rx.at[which, g],
                        device_id={"head": other},
                        device_id_type=MESH,
                    ).start()
            for which in kinds:
                pltpu.make_async_copy(
                    (k_ref, v_ref, q_ref)[which].at[:, :, head_columns(me_h, g)],
                    landing(which, g).at[:, token_rows(me_h), :],
                    rx.at[which, g],
                ).start()

        def await_bytes(ref, sem):
            pltpu.make_async_copy(ref, ref, sem).wait()

        def send_window(which, window, g, t):
            own = window[g].at[tiles + t]
            for side, (other, inside) in enumerate(ctx_sides):
                @pl.when(inside)
                def _():
                    pltpu.make_async_remote_copy(
                        src_ref=own,
                        dst_ref=window[g].at[2 * tiles * side + t],
                        send_sem=wtx.at[which, side, g],
                        recv_sem=win.at[which, g],
                        device_id={"ctx": other},
                        device_id_type=MESH,
                    ).start()

                @pl.when(jnp.logical_not(inside))
                def _():
                    pltpu.make_async_copy(
                        own, window[g].at[2 * tiles * (1 - side) + t], win.at[which, g]
                    ).start()

        def share_keys(g):
            await_bytes(landing(0, g), rx.at[0, g])

            def pass_on(t, carry):
                kwin[g][tiles + t] = k_all[g, t].T
                send_window(0, kwin, g, t)
                return carry

            lax.fori_loop(0, tiles, pass_on, 0)

        def share_values(g):
            await_bytes(landing(1, g), rx.at[1, g])

            def pass_on(t, carry):
                send_window(1, vwin, g, t)
                return carry

            lax.fori_loop(0, tiles, pass_on, 0)

        def pair_of(t, p):
            slot = jnp.clip(slots_ref[t, p] - first_slot, 0, 3 * tiles - 1)
            return slot, jnp.where(p < count_ref[t], 0.0, MASKED).astype(jnp.float32)

        def step(g, done, coming):
            if coming is not None:
                t_in, side_in = coming
                query = q_all[g, t_in]
                top_in = jnp.full((tok, DH), -MASKED, jnp.float32)
            if done is not None:
                t_out, side_out = done
                top_out = tops[side_out][...]
                merged = jnp.zeros((tok, 2 * DH), jnp.float32)
                ones = jnp.ones((2 * tok, DH), jnp.bfloat16)
            for p in range(0, most, 2):
                if coming is not None:
                    (slot0, shift0), (slot1, shift1) = pair_of(t_in, p), pair_of(t_in, p + 1)
                    keys = jnp.concatenate([kwin[g][slot0], kwin[g][slot1]], axis=1)
                    both = jnp.dot(query, keys, preferred_element_type=jnp.float32)
                    score_bufs[side_in][:, p * tok:(p + 2) * tok] = both
                    for start, shift in ((0, shift0), (tok, shift1)):
                        most_of = both[:, start:start + DH]
                        for at in range(start + DH, start + tok, DH):
                            most_of = jnp.maximum(most_of, both[:, at:at + DH])
                        top_in = jnp.maximum(top_in, most_of - shift)
                if done is not None:
                    (slot0, shift0), (slot1, shift1) = pair_of(t_out, p), pair_of(t_out, p + 1)
                    weights = []
                    for start, shift in ((p * tok, shift0), ((p + 1) * tok, shift1)):
                        base = top_out + shift
                        for at in range(start, start + tok, DH):
                            s = score_bufs[side_out][:, at:at + DH]
                            weights.append(jnp.exp2(s * EXP2_SCALE - base).astype(jnp.bfloat16))
                    values = jnp.concatenate([vwin[g][slot0], vwin[g][slot1]], axis=0)
                    merged = merged + jnp.dot(
                        jnp.concatenate(weights, axis=1),
                        jnp.concatenate([values, ones], axis=1),
                        preferred_element_type=jnp.float32,
                    )
            if coming is not None:
                top_in = jnp.max(top_in, axis=1, keepdims=True) * EXP2_SCALE
                tops[side_in][...] = jnp.broadcast_to(top_in, (tok, DH))
            if done is not None:
                o_all[g, t_out] = (merged[:, :DH] / merged[:, DH:]).astype(jnp.bfloat16)

        def compute(g, duties):
            def finish(t):
                if g == heads - 1:
                    send_output(g, t)
                for at, duty in duties:
                    pl.when(t == at)(duty)

            def two_tiles(i, carry):
                step(g, (2 * i, 0), (2 * i + 1, 1))
                finish(2 * i)
                last = i == tiles // 2 - 1
                pl.when(last)(functools.partial(step, g, (2 * i + 1, 1), None))
                pl.when(jnp.logical_not(last))(
                    functools.partial(step, g, (2 * i + 1, 1), (jnp.minimum(2 * i + 2, tiles - 1), 0))
                )
                finish(2 * i + 1)
                return carry

            step(g, None, (0, 0))
            lax.fori_loop(0, tiles // 2, two_tiles, 0)

        def send_output(g, ts):
            target = out_ref.at[ts, :, head_columns(me_h, g)]
            for other in others:
                pltpu.make_async_remote_copy(
                    src_ref=o_all.at[g, ts, token_rows(other), :],
                    dst_ref=target,
                    send_sem=o_tx.at[g],
                    recv_sem=o_rx.at[g],
                    device_id={"head": other},
                    device_id_type=MESH,
                ).start()
            pltpu.make_async_copy(
                o_all.at[g, ts, token_rows(me_h), :], target, o_rx.at[g]
            ).start()

        def send_outputs(g):
            send_output(g, slice(None))

        def later(duty, *args):
            return functools.partial(duty, *args) if args[-1] < heads else lambda: None

        send_inputs((0, 1, 2), 0)
        later(send_inputs, (0, 1), 1)()
        list_copies = [
            pltpu.make_async_copy(source, target, lists.at[i])
            for i, (source, target) in enumerate(((slots_hbm, slots_ref), (count_hbm, count_ref)))
        ]
        for copy in list_copies:
            copy.start()
        share_keys(0)
        share_values(0)
        later(send_inputs, (2,), 1)()
        later(send_inputs, (0, 1), 2)()
        for copy in list_copies:
            copy.wait()
        for g in range(heads):
            duties = [(0, later(send_inputs, (0, 1), g + 3)), (0, later(send_inputs, (2,), g + 2))]
            sharing = [(0, later(share_keys, g + 1)), (1, later(share_values, g + 1))]
            if g < heads // 2:
                duties = sharing + duties
            else:
                for _, duty in sharing:
                    duty()
            if g == heads - 2:
                duties += [(min(held, tiles - 1), later(send_outputs, held)) for held in range(g)]
            elif g == heads - 1 and g > 0:
                duties.append((0, later(send_outputs, g - 1)))
            await_bytes(q_all.at[g], rx.at[2, g])
            await_bytes(kwin[g].at[:2 * tiles], win.at[0, g])
            await_bytes(vwin[g].at[:2 * tiles], win.at[1, g])
            compute(g, duties)

        sent = tiles * (n_head - 1) // n_head
        for which, source in enumerate((k_ref, v_ref, q_ref)):
            await_bytes(source.at[:sent], tx.at[which])
        for g in range(heads):
            for which, window in enumerate((kwin, vwin)):
                for side, (_, inside) in enumerate(ctx_sides):
                    pl.when(inside)(
                        functools.partial(await_bytes, window[g].at[:tiles], wtx.at[which, side, g])
                    )
            await_bytes(o_all.at[g, :, :(n_head - 1) * rows, :], o_tx.at[g])
            await_bytes(o_all.at[g], o_rx.at[g])

    return kernel


def solution(mesh):
    n_head, n_ctx = mesh.shape["head"], mesh.shape["ctx"]

    def body(query, keys_in, values_in, pair_keys, pair_count):
        tiles, rows, width = query.shape
        most = pair_keys.shape[1]
        tok, heads = rows * n_head, width // DH // n_head
        units = tiles * most * heads
        dma = pltpu.SemaphoreType.DMA
        scratch = [pltpu.VMEM((3 * tiles, DH, tok), jnp.bfloat16)] * heads
        scratch += [pltpu.VMEM((3 * tiles, tok, DH), jnp.bfloat16)] * heads
        scratch += [pltpu.VMEM((heads, tiles, tok, DH), jnp.bfloat16)] * 3
        scratch += [pltpu.VMEM((tok, most * tok), jnp.float32)] * 2
        scratch += [pltpu.VMEM((tok, DH), jnp.float32)] * 2
        scratch += [pltpu.SMEM(pair_keys.shape, jnp.int32), pltpu.SMEM(pair_count.shape, jnp.int32)]
        scratch += [dma((3, heads)), dma((3,)), dma((2, heads)), dma((2, 2, heads)), dma((heads,)), dma((heads,)), dma((2,))]
        in_hbm = pl.BlockSpec(memory_space=pltpu.HBM)
        return pl.pallas_call(
            build_kernel(n_head, n_ctx, tiles, rows, heads, most),
            out_shape=pltpu.VMEM(query.shape, query.dtype),
            in_specs=[in_hbm] * 5,
            out_specs=pl.BlockSpec(memory_space=pltpu.VMEM),
            scratch_shapes=scratch,
            compiler_params=pltpu.CompilerParams(
                collective_id=0, has_side_effects=True, vmem_limit_bytes=60 * 2 ** 20
            ),
            cost_estimate=pl.CostEstimate(
                flops=units * 4 * tok * tok * DH,
                bytes_accessed=8 * query.size,
                transcendentals=units * tok * tok,
            ),
        )(pair_keys, pair_count, query, keys_in, values_in)

    tokens = P("ctx", "head", None)
    return jax.shard_map(
        body,
        mesh=mesh,
        in_specs=(tokens, tokens, tokens, P("ctx", None), P("ctx")),
        out_specs=tokens,
        check_vma=False,
    )
```

```python
import functools

import jax
import jax.numpy as jnp
from jax import lax
from jax.experimental import pallas as pl
from jax.experimental.pallas import tpu as pltpu
from jax.sharding import PartitionSpec as P

DH = 128
EXP2_SCALE = DH ** -0.5 * 1.4426950408889634
MASKED = 1e30
MESH = pl.DeviceIdType.MESH


def build_kernel(n_head, n_ctx, tiles, rows, heads, most):
    tok = n_head * rows

    def kernel(slots_hbm, count_hbm, q_ref, k_ref, v_ref, out_ref, *scratch):
        kwin, vwin = scratch[:heads], scratch[heads:2 * heads]
        q_all, k_all, o_all, *rest = scratch[2 * heads:]
        staged, staging = rest.pop(), rest.pop()
        score_bufs, tops = rest[:2], rest[2:4]
        slots_ref, count_ref = rest[4:6]
        rx, tx, win, wtx, o_rx, o_tx, lists = rest[6:]
        me_h, me_c = lax.axis_index("head"), lax.axis_index("ctx")
        first_slot = (me_c - 1) * tiles
        others = [lax.rem(me_h + step, n_head) for step in (1, n_head - 1, *range(2, n_head - 1))]

        stage_copies = [
            pltpu.make_async_copy(source, staged.at[which], staging.at[which])
            for which, source in enumerate((k_ref, v_ref, q_ref))
        ]
        for copy in stage_copies:
            copy.start()
        barrier = pltpu.get_barrier_semaphore()
        for other in others:
            pl.semaphore_signal(barrier, inc=1, device_id={"head": other}, device_id_type=MESH)
        ctx_sides = ((me_c + 1, me_c < n_ctx - 1), (me_c - 1, me_c > 0))
        for other, inside in ctx_sides:
            @pl.when(inside)
            def _():
                pl.semaphore_signal(barrier, inc=1, device_id={"ctx": other}, device_id_type=MESH)
        at_edge = jnp.logical_or(me_c == 0, me_c == n_ctx - 1)
        for edge, partners in ((at_edge, len(others) + 1), (jnp.logical_not(at_edge), len(others) + 2)):
            pl.when(edge)(functools.partial(pl.semaphore_wait, barrier, partners))

        def head_columns(owner, g):
            return pl.ds(pl.multiple_of((owner * heads + g) * DH, DH), DH)

        def token_rows(owner):
            return pl.ds(pl.multiple_of(owner * rows, rows), rows)

        def landing(which, g):
            if which == 1:
                return vwin[g].at[tiles:2 * tiles]
            return (k_all if which == 0 else q_all).at[g]

        def send_inputs(kinds, g):
            for which in kinds:
                source = staged.at[which] if g > 0 else (k_ref, v_ref, q_ref)[which]
                target = landing(which, g).at[:, token_rows(me_h), :]
                for other in others:
                    pltpu.make_async_remote_copy(
                        src_ref=source.at[:, :, head_columns(other, g)],
                        dst_ref=target,
                        send_sem=tx.at[which],
                        recv_sem=rx.at[which, g],
                        device_id={"head": other},
                        device_id_type=MESH,
                    ).start()
            for which in kinds:
                pltpu.make_async_copy(
                    (staged.at[which] if g > 0 else (k_ref, v_ref, q_ref)[which]).at[:, :, head_columns(me_h, g)],
                    landing(which, g).at[:, token_rows(me_h), :],
                    rx.at[which, g],
                ).start()

        def await_bytes(ref, sem):
            pltpu.make_async_copy(ref, ref, sem).wait()

        def send_window(which, window, g, t):
            own = window[g].at[tiles + t]
            for side, (other, inside) in enumerate(ctx_sides):
                @pl.when(inside)
                def _():
                    pltpu.make_async_remote_copy(
                        src_ref=own,
                        dst_ref=window[g].at[2 * tiles * side + t],
                        send_sem=wtx.at[which, side, g],
                        recv_sem=win.at[which, g],
                        device_id={"ctx": other},
                        device_id_type=MESH,
                    ).start()

                @pl.when(jnp.logical_not(inside))
                def _():
                    pltpu.make_async_copy(
                        own, window[g].at[2 * tiles * (1 - side) + t], win.at[which, g]
                    ).start()

        def share_keys(g):
            await_bytes(landing(0, g), rx.at[0, g])

            def pass_on(t, carry):
                kwin[g][tiles + t] = k_all[g, t].T
                send_window(0, kwin, g, t)
                return carry

            lax.fori_loop(0, tiles, pass_on, 0)

        def share_values(g):
            await_bytes(landing(1, g), rx.at[1, g])

            def pass_on(t, carry):
                send_window(1, vwin, g, t)
                return carry

            lax.fori_loop(0, tiles, pass_on, 0)

        half = tok // 2

        def pair_of(t, p):
            slot = jnp.clip(slots_ref[t, p] - first_slot, 0, 3 * tiles - 1)
            return slot, jnp.where(p < count_ref[t], 0.0, MASKED).astype(jnp.float32)

        def half_step(g, done, coming):
            if coming is not None:
                t_in, side_in = coming
                query = q_all[g, t_in, side_in * half:(side_in + 1) * half]
                top_in = jnp.full((half, DH), -MASKED, jnp.float32)
            if done is not None:
                t_out, side_out = done
                top_out = tops[side_out][...]
                merged = jnp.zeros((half, 2 * DH), jnp.float32)
                ones = jnp.ones((2 * tok, DH), jnp.bfloat16)
            for p in range(0, most, 2):
                if coming is not None:
                    (slot0, shift0), (slot1, shift1) = pair_of(t_in, p), pair_of(t_in, p + 1)
                    keys = jnp.concatenate([kwin[g][slot0], kwin[g][slot1]], axis=1)
                    both = jnp.dot(query, keys, preferred_element_type=jnp.float32)
                    score_bufs[side_in][:, p * tok:(p + 2) * tok] = both
                    for start, shift in ((0, shift0), (tok, shift1)):
                        most_of = both[:, start:start + DH]
                        for at in range(start + DH, start + tok, DH):
                            most_of = jnp.maximum(most_of, both[:, at:at + DH])
                        top_in = jnp.maximum(top_in, most_of - shift)
                if done is not None:
                    (slot0, shift0), (slot1, shift1) = pair_of(t_out, p), pair_of(t_out, p + 1)
                    weights = []
                    for start, shift in ((p * tok, shift0), ((p + 1) * tok, shift1)):
                        base = top_out + shift
                        for at in range(start, start + tok, DH):
                            s = score_bufs[side_out][:, at:at + DH]
                            weights.append(jnp.exp2(s * EXP2_SCALE - base).astype(jnp.bfloat16))
                    values = jnp.concatenate([vwin[g][slot0], vwin[g][slot1]], axis=0)
                    merged = merged + jnp.dot(
                        jnp.concatenate(weights, axis=1),
                        jnp.concatenate([values, ones], axis=1),
                        preferred_element_type=jnp.float32,
                    )
            if coming is not None:
                top_in = jnp.max(top_in, axis=1, keepdims=True) * EXP2_SCALE
                tops[side_in][...] = jnp.broadcast_to(top_in, (half, DH))
            if done is not None:
                o_all[g, t_out, side_out * half:(side_out + 1) * half] = (
                    merged[:, :DH] / merged[:, DH:]
                ).astype(jnp.bfloat16)

        def compute(g, duties):
            def one_tile(t, carry):
                half_step(g, (t, 0), (t, 1))
                half_step(g, (t, 1), (jnp.minimum(t + 1, tiles - 1), 0))
                if g == heads - 1:
                    send_output(g, t)
                for at, duty in duties:
                    pl.when(t == at)(duty)
                return carry

            half_step(g, None, (0, 0))
            lax.fori_loop(0, tiles, one_tile, 0)

        def send_output(g, ts):
            target = out_ref.at[ts, :, head_columns(me_h, g)]
            for other in others:
                pltpu.make_async_remote_copy(
                    src_ref=o_all.at[g, ts, token_rows(other), :],
                    dst_ref=target,
                    send_sem=o_tx.at[g],
                    recv_sem=o_rx.at[g],
                    device_id={"head": other},
                    device_id_type=MESH,
                ).start()
            pltpu.make_async_copy(
                o_all.at[g, ts, token_rows(me_h), :], target, o_rx.at[g]
            ).start()

        def send_outputs(g):
            send_output(g, slice(None))

        def later(duty, *args):
            return functools.partial(duty, *args) if args[-1] < heads else lambda: None

        send_inputs((0, 1, 2), 0)
        for copy in stage_copies:
            copy.wait()
        later(send_inputs, (0, 1), 1)()
        list_copies = [
            pltpu.make_async_copy(source, target, lists.at[i])
            for i, (source, target) in enumerate(((slots_hbm, slots_ref), (count_hbm, count_ref)))
        ]
        for copy in list_copies:
            copy.start()
        share_keys(0)
        share_values(0)
        later(send_inputs, (2,), 1)()
        later(send_inputs, (0, 1), 2)()
        for copy in list_copies:
            copy.wait()
        for g in range(heads):
            duties = [(0, later(send_inputs, (0, 1), g + 3)), (0, later(send_inputs, (2,), g + 2))]
            sharing = [(0, later(share_keys, g + 1)), (1, later(share_values, g + 1))]
            if g < heads // 2:
                duties = sharing + duties
            else:
                for _, duty in sharing:
                    duty()
            if g == heads - 2:
                duties += [(min(held, tiles - 1), later(send_outputs, held)) for held in range(g)]
            elif g == heads - 1 and g > 0:
                duties.append((0, later(send_outputs, g - 1)))
            await_bytes(q_all.at[g], rx.at[2, g])
            await_bytes(kwin[g].at[:2 * tiles], win.at[0, g])
            await_bytes(vwin[g].at[:2 * tiles], win.at[1, g])
            compute(g, duties)

        sent = tiles * (n_head - 1) // n_head
        for which, source in enumerate((k_ref, v_ref, q_ref)):
            await_bytes(source.at[:sent], tx.at[which])
        for g in range(heads):
            for which, window in enumerate((kwin, vwin)):
                for side, (_, inside) in enumerate(ctx_sides):
                    pl.when(inside)(
                        functools.partial(await_bytes, window[g].at[:tiles], wtx.at[which, side, g])
                    )
            await_bytes(o_all.at[g, :, :(n_head - 1) * rows, :], o_tx.at[g])
            await_bytes(o_all.at[g], o_rx.at[g])

    return kernel


def solution(mesh):
    n_head, n_ctx = mesh.shape["head"], mesh.shape["ctx"]

    def body(query, keys_in, values_in, pair_keys, pair_count):
        tiles, rows, width = query.shape
        most = pair_keys.shape[1]
        tok, heads = rows * n_head, width // DH // n_head
        units = tiles * most * heads
        dma = pltpu.SemaphoreType.DMA
        scratch = [pltpu.VMEM((3 * tiles, DH, tok), jnp.bfloat16)] * heads
        scratch += [pltpu.VMEM((3 * tiles, tok, DH), jnp.bfloat16)] * heads
        scratch += [pltpu.VMEM((heads, tiles, tok, DH), jnp.bfloat16)] * 3
        scratch += [pltpu.VMEM((tok // 2, most * tok), jnp.float32)] * 2
        scratch += [pltpu.VMEM((tok // 2, DH), jnp.float32)] * 2
        scratch += [pltpu.SMEM(pair_keys.shape, jnp.int32), pltpu.SMEM(pair_count.shape, jnp.int32)]
        scratch += [dma((3, heads)), dma((3,)), dma((2, heads)), dma((2, 2, heads)), dma((heads,)), dma((heads,)), dma((2,))]
        scratch += [dma((3,)), pltpu.VMEM((3, *query.shape), jnp.bfloat16)]
        in_hbm = pl.BlockSpec(memory_space=pltpu.HBM)
        return pl.pallas_call(
            build_kernel(n_head, n_ctx, tiles, rows, heads, most),
            out_shape=pltpu.VMEM(query.shape, query.dtype),
            in_specs=[in_hbm] * 5,
            out_specs=pl.BlockSpec(memory_space=pltpu.VMEM),
            scratch_shapes=scratch,
            compiler_params=pltpu.CompilerParams(
                collective_id=0, has_side_effects=True, vmem_limit_bytes=60 * 2 ** 20
            ),
            cost_estimate=pl.CostEstimate(
                flops=units * 4 * tok * tok * DH,
                bytes_accessed=8 * query.size,
                transcendentals=units * tok * tok,
            ),
        )(pair_keys, pair_count, query, keys_in, values_in)

    tokens = P("ctx", "head", None)
    return jax.shard_map(
        body,
        mesh=mesh,
        in_specs=(tokens, tokens, tokens, P("ctx", None), P("ctx")),
        out_specs=tokens,
        check_vma=False,
    )
```

```python
import functools

import jax
import jax.numpy as jnp
from jax import lax
from jax.experimental import pallas as pl
from jax.experimental.pallas import tpu as pltpu
from jax.sharding import PartitionSpec as P

DH = 128
EXP2_SCALE = DH ** -0.5 * 1.4426950408889634
MASKED = 1e30
MESH = pl.DeviceIdType.MESH


def build_kernel(n_head, n_ctx, tiles, rows, heads, most):
    tok = n_head * rows

    def kernel(slots_hbm, count_hbm, q_ref, k_ref, v_ref, out_ref, *scratch):
        kwin, vwin = scratch[:heads], scratch[heads:2 * heads]
        q_all, k_all, o_all, *rest = scratch[2 * heads:]
        score_bufs, tops = rest[:2], rest[2:4]
        slots_ref, count_ref = rest[4:6]
        rx, tx, win, wtx, o_rx, o_tx, lists = rest[6:]
        me_h, me_c = lax.axis_index("head"), lax.axis_index("ctx")
        first_slot = (me_c - 1) * tiles
        others = [lax.rem(me_h + step, n_head) for step in (*range(2, n_head - 1), 1, n_head - 1)]

        barrier = pltpu.get_barrier_semaphore()
        for other in others:
            pl.semaphore_signal(barrier, inc=1, device_id={"head": other}, device_id_type=MESH)
        ctx_sides = ((me_c + 1, me_c < n_ctx - 1), (me_c - 1, me_c > 0))
        for other, inside in ctx_sides:
            @pl.when(inside)
            def _():
                pl.semaphore_signal(barrier, inc=1, device_id={"ctx": other}, device_id_type=MESH)
        at_edge = jnp.logical_or(me_c == 0, me_c == n_ctx - 1)
        for edge, partners in ((at_edge, len(others) + 1), (jnp.logical_not(at_edge), len(others) + 2)):
            pl.when(edge)(functools.partial(pl.semaphore_wait, barrier, partners))

        def head_columns(owner, g):
            return pl.ds(pl.multiple_of((owner * heads + g) * DH, DH), DH)

        def token_rows(owner):
            return pl.ds(pl.multiple_of(owner * rows, rows), rows)

        def landing(which, g):
            if which == 1:
                return vwin[g].at[tiles:2 * tiles]
            return (k_all if which == 0 else q_all).at[g]

        def send_inputs(kinds, g):
            for which in kinds:
                source = (k_ref, v_ref, q_ref)[which]
                target = landing(which, g).at[:, token_rows(me_h), :]
                for other in others:
                    pltpu.make_async_remote_copy(
                        src_ref=source.at[:, :, head_columns(other, g)],
                        dst_ref=target,
                        send_sem=tx.at[which],
                        recv_sem=rx.at[which, g],
                        device_id={"head": other},
                        device_id_type=MESH,
                    ).start()
            for which in kinds:
                pltpu.make_async_copy(
                    (k_ref, v_ref, q_ref)[which].at[:, :, head_columns(me_h, g)],
                    landing(which, g).at[:, token_rows(me_h), :],
                    rx.at[which, g],
                ).start()

        def await_bytes(ref, sem):
            pltpu.make_async_copy(ref, ref, sem).wait()

        def send_window(which, window, g, t):
            own = window[g].at[tiles + t]
            for side, (other, inside) in enumerate(ctx_sides):
                @pl.when(inside)
                def _():
                    pltpu.make_async_remote_copy(
                        src_ref=own,
                        dst_ref=window[g].at[2 * tiles * side + t],
                        send_sem=wtx.at[which, side, g],
                        recv_sem=win.at[which, g],
                        device_id={"ctx": other},
                        device_id_type=MESH,
                    ).start()

                @pl.when(jnp.logical_not(inside))
                def _():
                    pltpu.make_async_copy(
                        own, window[g].at[2 * tiles * (1 - side) + t], win.at[which, g]
                    ).start()

        def share_keys(g):
            await_bytes(landing(0, g), rx.at[0, g])

            def pass_on(t, carry):
                kwin[g][tiles + t] = k_all[g, t].T
                send_window(0, kwin, g, t)
                return carry

            lax.fori_loop(0, tiles, pass_on, 0)

        def share_values(g):
            await_bytes(landing(1, g), rx.at[1, g])

            def pass_on(t, carry):
                send_window(1, vwin, g, t)
                return carry

            lax.fori_loop(0, tiles, pass_on, 0)

        half = tok // 2

        def pair_of(t, p):
            slot = jnp.clip(slots_ref[t, p] - first_slot, 0, 3 * tiles - 1)
            return slot, jnp.where(p < count_ref[t], 0.0, MASKED).astype(jnp.float32)

        def half_step(g, done, coming):
            if coming is not None:
                t_in, side_in = coming
                query = q_all[g, t_in, side_in * half:(side_in + 1) * half]
                top_in = jnp.full((half, DH), -MASKED, jnp.float32)
            if done is not None:
                t_out, side_out = done
                top_out = tops[side_out][...]
                merged = jnp.zeros((half, 2 * DH), jnp.float32)
                ones = jnp.ones((2 * tok, DH), jnp.bfloat16)
            for p in range(0, most, 2):
                if coming is not None:
                    (slot0, shift0), (slot1, shift1) = pair_of(t_in, p), pair_of(t_in, p + 1)
                    keys = jnp.concatenate([kwin[g][slot0], kwin[g][slot1]], axis=1)
                    both = jnp.dot(query, keys, preferred_element_type=jnp.float32)
                    score_bufs[side_in][:, p * tok:(p + 2) * tok] = both
                    for start, shift in ((0, shift0), (tok, shift1)):
                        most_of = both[:, start:start + DH]
                        for at in range(start + DH, start + tok, DH):
                            most_of = jnp.maximum(most_of, both[:, at:at + DH])
                        top_in = jnp.maximum(top_in, most_of - shift)
                if done is not None:
                    (slot0, shift0), (slot1, shift1) = pair_of(t_out, p), pair_of(t_out, p + 1)
                    weights = []
                    for start, shift in ((p * tok, shift0), ((p + 1) * tok, shift1)):
                        base = top_out + shift
                        for at in range(start, start + tok, DH):
                            s = score_bufs[side_out][:, at:at + DH]
                            weights.append(jnp.exp2(s * EXP2_SCALE - base).astype(jnp.bfloat16))
                    values = jnp.concatenate([vwin[g][slot0], vwin[g][slot1]], axis=0)
                    merged = merged + jnp.dot(
                        jnp.concatenate(weights, axis=1),
                        jnp.concatenate([values, ones], axis=1),
                        preferred_element_type=jnp.float32,
                    )
            if coming is not None:
                top_in = jnp.max(top_in, axis=1, keepdims=True) * EXP2_SCALE
                tops[side_in][...] = jnp.broadcast_to(top_in, (half, DH))
            if done is not None:
                o_all[g, t_out, side_out * half:(side_out + 1) * half] = (
                    merged[:, :DH] / merged[:, DH:]
                ).astype(jnp.bfloat16)

        def compute(g, duties):
            def one_tile(t, carry):
                half_step(g, (t, 0), (t, 1))
                half_step(g, (t, 1), (jnp.minimum(t + 1, tiles - 1), 0))
                if g == heads - 1:
                    send_output(g, t)
                for at, duty in duties:
                    pl.when(t == at)(duty)
                return carry

            half_step(g, None, (0, 0))
            lax.fori_loop(0, tiles, one_tile, 0)

        def send_output(g, ts):
            target = out_ref.at[ts, :, head_columns(me_h, g)]
            for other in others:
                pltpu.make_async_remote_copy(
                    src_ref=o_all.at[g, ts, token_rows(other), :],
                    dst_ref=target,
                    send_sem=o_tx.at[g],
                    recv_sem=o_rx.at[g],
                    device_id={"head": other},
                    device_id_type=MESH,
                ).start()
            pltpu.make_async_copy(
                o_all.at[g, ts, token_rows(me_h), :], target, o_rx.at[g]
            ).start()

        def send_outputs(g):
            send_output(g, slice(None))

        def later(duty, *args):
            return functools.partial(duty, *args) if args[-1] < heads else lambda: None

        send_inputs((0, 1, 2), 0)
        later(send_inputs, (0, 1), 1)()
        list_copies = [
            pltpu.make_async_copy(source, target, lists.at[i])
            for i, (source, target) in enumerate(((slots_hbm, slots_ref), (count_hbm, count_ref)))
        ]
        for copy in list_copies:
            copy.start()
        share_keys(0)
        share_values(0)
        later(send_inputs, (2,), 1)()
        later(send_inputs, (0, 1), 2)()
        for copy in list_copies:
            copy.wait()
        for g in range(heads):
            duties = [(0, later(send_inputs, (0, 1), g + 3)), (0, later(send_inputs, (2,), g + 2))]
            sharing = [(0, later(share_keys, g + 1)), (1, later(share_values, g + 1))]
            if g < heads // 2:
                duties = sharing + duties
            else:
                for _, duty in sharing:
                    duty()
            if g == heads - 2:
                duties += [(min(held, tiles - 1), later(send_outputs, held)) for held in range(g)]
            elif g == heads - 1 and g > 0:
                duties.append((0, later(send_outputs, g - 1)))
            await_bytes(q_all.at[g], rx.at[2, g])
            await_bytes(kwin[g].at[:2 * tiles], win.at[0, g])
            await_bytes(vwin[g].at[:2 * tiles], win.at[1, g])
            compute(g, duties)

        sent = tiles * (n_head - 1) // n_head
        for which, source in enumerate((k_ref, v_ref, q_ref)):
            await_bytes(source.at[:sent], tx.at[which])
        for g in range(heads):
            for which, window in enumerate((kwin, vwin)):
                for side, (_, inside) in enumerate(ctx_sides):
                    pl.when(inside)(
                        functools.partial(await_bytes, window[g].at[:tiles], wtx.at[which, side, g])
                    )
            await_bytes(o_all.at[g, :, :(n_head - 1) * rows, :], o_tx.at[g])
            await_bytes(o_all.at[g], o_rx.at[g])

    return kernel


def solution(mesh):
    n_head, n_ctx = mesh.shape["head"], mesh.shape["ctx"]

    def body(query, keys_in, values_in, pair_keys, pair_count):
        tiles, rows, width = query.shape
        most = pair_keys.shape[1]
        tok, heads = rows * n_head, width // DH // n_head
        units = tiles * most * heads
        dma = pltpu.SemaphoreType.DMA
        scratch = [pltpu.VMEM((3 * tiles, DH, tok), jnp.bfloat16)] * heads
        scratch += [pltpu.VMEM((3 * tiles, tok, DH), jnp.bfloat16)] * heads
        scratch += [pltpu.VMEM((heads, tiles, tok, DH), jnp.bfloat16)] * 3
        scratch += [pltpu.VMEM((tok // 2, most * tok), jnp.float32)] * 2
        scratch += [pltpu.VMEM((tok // 2, DH), jnp.float32)] * 2
        scratch += [pltpu.SMEM(pair_keys.shape, jnp.int32), pltpu.SMEM(pair_count.shape, jnp.int32)]
        scratch += [dma((3, heads)), dma((3,)), dma((2, heads)), dma((2, 2, heads)), dma((heads,)), dma((heads,)), dma((2,))]
        in_hbm = pl.BlockSpec(memory_space=pltpu.HBM)
        return pl.pallas_call(
            build_kernel(n_head, n_ctx, tiles, rows, heads, most),
            out_shape=pltpu.VMEM(query.shape, query.dtype),
            in_specs=[in_hbm] * 5,
            out_specs=pl.BlockSpec(memory_space=pltpu.VMEM),
            scratch_shapes=scratch,
            compiler_params=pltpu.CompilerParams(
                collective_id=0, has_side_effects=True, vmem_limit_bytes=60 * 2 ** 20
            ),
            cost_estimate=pl.CostEstimate(
                flops=units * 4 * tok * tok * DH,
                bytes_accessed=8 * query.size,
                transcendentals=units * tok * tok,
            ),
        )(pair_keys, pair_count, query, keys_in, values_in)

    tokens = P("ctx", "head", None)
    return jax.shard_map(
        body,
        mesh=mesh,
        in_specs=(tokens, tokens, tokens, P("ctx", None), P("ctx")),
        out_specs=tokens,
        check_vma=False,
    )
```

```python
import functools

import jax
import jax.numpy as jnp
from jax import lax
from jax.experimental import pallas as pl
from jax.experimental.pallas import tpu as pltpu
from jax.sharding import PartitionSpec as P

DH = 128
EXP2_SCALE = DH ** -0.5 * 1.4426950408889634
MASKED = 1e30
MESH = pl.DeviceIdType.MESH


def build_kernel(n_head, n_ctx, tiles, rows, heads, most):
    tok = n_head * rows

    def kernel(slots_hbm, count_hbm, q_ref, k_ref, v_ref, out_ref, *scratch):
        kwin, vwin = scratch[:heads], scratch[heads:2 * heads]
        q_all, k_all, o_all, *rest = scratch[2 * heads:]
        score_bufs, tops = rest[:2], rest[2:4]
        slots_ref, count_ref = rest[4:6]
        rx, tx, win, wtx, o_rx, o_tx, lists = rest[6:]
        me_h, me_c = lax.axis_index("head"), lax.axis_index("ctx")
        first_slot = (me_c - 1) * tiles
        others = [lax.rem(me_h + step, n_head) for step in (*range(2, n_head - 1), 1, n_head - 1)]

        barrier = pltpu.get_barrier_semaphore()
        for other in others:
            pl.semaphore_signal(barrier, inc=1, device_id={"head": other}, device_id_type=MESH)
        ctx_sides = ((me_c + 1, me_c < n_ctx - 1), (me_c - 1, me_c > 0))
        for other, inside in ctx_sides:
            @pl.when(inside)
            def _():
                pl.semaphore_signal(barrier, inc=1, device_id={"ctx": other}, device_id_type=MESH)
        at_edge = jnp.logical_or(me_c == 0, me_c == n_ctx - 1)
        for edge, partners in ((at_edge, len(others) + 1), (jnp.logical_not(at_edge), len(others) + 2)):
            pl.when(edge)(functools.partial(pl.semaphore_wait, barrier, partners))

        def head_columns(owner, g):
            return pl.ds(pl.multiple_of((owner * heads + g) * DH, DH), DH)

        def token_rows(owner):
            return pl.ds(pl.multiple_of(owner * rows, rows), rows)

        def landing(which, g):
            if which == 1:
                return vwin[g].at[tiles:2 * tiles]
            return (k_all if which == 0 else q_all).at[g]

        def send_inputs(kinds, g):
            for which in kinds:
                source = (k_ref, v_ref, q_ref)[which]
                target = landing(which, g).at[:, token_rows(me_h), :]
                for other in others:
                    pltpu.make_async_remote_copy(
                        src_ref=source.at[:, :, head_columns(other, g)],
                        dst_ref=target,
                        send_sem=tx.at[which],
                        recv_sem=rx.at[which, g],
                        device_id={"head": other},
                        device_id_type=MESH,
                    ).start()
            for which in kinds:
                pltpu.make_async_copy(
                    (k_ref, v_ref, q_ref)[which].at[:, :, head_columns(me_h, g)],
                    landing(which, g).at[:, token_rows(me_h), :],
                    rx.at[which, g],
                ).start()

        def await_bytes(ref, sem):
            pltpu.make_async_copy(ref, ref, sem).wait()

        def send_window(which, window, g, t, count=1):
            own = window[g].at[pl.ds(tiles + t, count)]
            for side, (other, inside) in enumerate(ctx_sides):
                @pl.when(inside)
                def _():
                    pltpu.make_async_remote_copy(
                        src_ref=own,
                        dst_ref=window[g].at[pl.ds(2 * tiles * side + t, count)],
                        send_sem=wtx.at[which, side, g],
                        recv_sem=win.at[which, g],
                        device_id={"ctx": other},
                        device_id_type=MESH,
                    ).start()

                @pl.when(jnp.logical_not(inside))
                def _():
                    pltpu.make_async_copy(
                        own, window[g].at[pl.ds(2 * tiles * (1 - side) + t, count)], win.at[which, g]
                    ).start()

        def share_keys(g):
            await_bytes(landing(0, g), rx.at[0, g])

            def pass_on(t, carry):
                kwin[g][tiles + t] = k_all[g, t].T
                send_window(0, kwin, g, t)
                return carry

            lax.fori_loop(0, tiles, pass_on, 0)

        def share_values(g):
            await_bytes(landing(1, g), rx.at[1, g])
            send_window(1, vwin, g, 0, tiles)

        half = tok // 2

        def pair_of(t, p):
            slot = jnp.clip(slots_ref[t, p] - first_slot, 0, 3 * tiles - 1)
            return slot, jnp.where(p < count_ref[t], 0.0, MASKED).astype(jnp.float32)

        def half_step(g, done, coming):
            if coming is not None:
                t_in, side_in = coming
                query = q_all[g, t_in, side_in * half:(side_in + 1) * half]
                top_in = jnp.full((half, DH), -MASKED, jnp.float32)
            if done is not None:
                t_out, side_out = done
                top_out = tops[side_out][...]
                merged = jnp.zeros((half, 2 * DH), jnp.float32)
                ones = jnp.ones((2 * tok, DH), jnp.bfloat16)
            for p in range(0, most, 2):
                if coming is not None:
                    (slot0, shift0), (slot1, shift1) = pair_of(t_in, p), pair_of(t_in, p + 1)
                    keys = jnp.concatenate([kwin[g][slot0], kwin[g][slot1]], axis=1)
                    both = jnp.dot(query, keys, preferred_element_type=jnp.float32)
                    score_bufs[side_in][:, p * tok:(p + 2) * tok] = both
                    for start, shift in ((0, shift0), (tok, shift1)):
                        most_of = both[:, start:start + DH]
                        for at in range(start + DH, start + tok, DH):
                            most_of = jnp.maximum(most_of, both[:, at:at + DH])
                        top_in = jnp.maximum(top_in, most_of - shift)
                if done is not None:
                    (slot0, shift0), (slot1, shift1) = pair_of(t_out, p), pair_of(t_out, p + 1)
                    weights = []
                    for start, shift in ((p * tok, shift0), ((p + 1) * tok, shift1)):
                        base = top_out + shift
                        for at in range(start, start + tok, DH):
                            s = score_bufs[side_out][:, at:at + DH]
                            weights.append(jnp.exp2(s * EXP2_SCALE - base).astype(jnp.bfloat16))
                    values = jnp.concatenate([vwin[g][slot0], vwin[g][slot1]], axis=0)
                    merged = merged + jnp.dot(
                        jnp.concatenate(weights, axis=1),
                        jnp.concatenate([values, ones], axis=1),
                        preferred_element_type=jnp.float32,
                    )
            if coming is not None:
                top_in = jnp.max(top_in, axis=1, keepdims=True) * EXP2_SCALE
                tops[side_in][...] = jnp.broadcast_to(top_in, (half, DH))
            if done is not None:
                o_all[g, t_out, side_out * half:(side_out + 1) * half] = (
                    merged[:, :DH] / merged[:, DH:]
                ).astype(jnp.bfloat16)

        def compute(g, duties):
            def one_tile(t, carry):
                half_step(g, (t, 0), (t, 1))
                half_step(g, (t, 1), (jnp.minimum(t + 1, tiles - 1), 0))
                if g == heads - 1:
                    send_output(g, t)
                for at, duty in duties:
                    pl.when(t == at)(duty)
                return carry

            half_step(g, None, (0, 0))
            lax.fori_loop(0, tiles, one_tile, 0)

        def send_output(g, ts):
            target = out_ref.at[ts, :, head_columns(me_h, g)]
            for other in others:
                pltpu.make_async_remote_copy(
                    src_ref=o_all.at[g, ts, token_rows(other), :],
                    dst_ref=target,
                    send_sem=o_tx.at[g],
                    recv_sem=o_rx.at[g],
                    device_id={"head": other},
                    device_id_type=MESH,
                ).start()
            pltpu.make_async_copy(
                o_all.at[g, ts, token_rows(me_h), :], target, o_rx.at[g]
            ).start()

        def send_outputs(g):
            send_output(g, slice(None))

        def later(duty, *args):
            return functools.partial(duty, *args) if args[-1] < heads else lambda: None

        send_inputs((0, 1, 2), 0)
        later(send_inputs, (0, 1), 1)()
        list_copies = [
            pltpu.make_async_copy(source, target, lists.at[i])
            for i, (source, target) in enumerate(((slots_hbm, slots_ref), (count_hbm, count_ref)))
        ]
        for copy in list_copies:
            copy.start()
        share_keys(0)
        share_values(0)
        later(send_inputs, (2,), 1)()
        later(send_inputs, (0, 1), 2)()
        for copy in list_copies:
            copy.wait()
        for g in range(heads):
            duties = [(0, later(send_inputs, (0, 1), g + 3)), (0, later(send_inputs, (2,), g + 2))]
            sharing = [(0, later(share_keys, g + 1)), (1, later(share_values, g + 1))]
            if g < heads // 2:
                duties = sharing + duties
            else:
                for _, duty in sharing:
                    duty()
            if g == heads - 2:
                duties += [(min(held, tiles - 1), later(send_outputs, held)) for held in range(g)]
            elif g == heads - 1 and g > 0:
                duties.append((0, later(send_outputs, g - 1)))
            await_bytes(q_all.at[g], rx.at[2, g])
            await_bytes(kwin[g].at[:2 * tiles], win.at[0, g])
            await_bytes(vwin[g].at[:2 * tiles], win.at[1, g])
            compute(g, duties)

        sent = tiles * (n_head - 1) // n_head
        for which, source in enumerate((k_ref, v_ref, q_ref)):
            await_bytes(source.at[:sent], tx.at[which])
        for g in range(heads):
            for which, window in enumerate((kwin, vwin)):
                for side, (_, inside) in enumerate(ctx_sides):
                    pl.when(inside)(
                        functools.partial(await_bytes, window[g].at[:tiles], wtx.at[which, side, g])
                    )
            await_bytes(o_all.at[g, :, :(n_head - 1) * rows, :], o_tx.at[g])
            await_bytes(o_all.at[g], o_rx.at[g])

    return kernel


def solution(mesh):
    n_head, n_ctx = mesh.shape["head"], mesh.shape["ctx"]

    def body(query, keys_in, values_in, pair_keys, pair_count):
        tiles, rows, width = query.shape
        most = pair_keys.shape[1]
        tok, heads = rows * n_head, width // DH // n_head
        units = tiles * most * heads
        dma = pltpu.SemaphoreType.DMA
        scratch = [pltpu.VMEM((3 * tiles, DH, tok), jnp.bfloat16)] * heads
        scratch += [pltpu.VMEM((3 * tiles, tok, DH), jnp.bfloat16)] * heads
        scratch += [pltpu.VMEM((heads, tiles, tok, DH), jnp.bfloat16)] * 3
        scratch += [pltpu.VMEM((tok // 2, most * tok), jnp.float32)] * 2
        scratch += [pltpu.VMEM((tok // 2, DH), jnp.float32)] * 2
        scratch += [pltpu.SMEM(pair_keys.shape, jnp.int32), pltpu.SMEM(pair_count.shape, jnp.int32)]
        scratch += [dma((3, heads)), dma((3,)), dma((2, heads)), dma((2, 2, heads)), dma((heads,)), dma((heads,)), dma((2,))]
        in_hbm = pl.BlockSpec(memory_space=pltpu.HBM)
        return pl.pallas_call(
            build_kernel(n_head, n_ctx, tiles, rows, heads, most),
            out_shape=pltpu.VMEM(query.shape, query.dtype),
            in_specs=[in_hbm] * 5,
            out_specs=pl.BlockSpec(memory_space=pltpu.VMEM),
            scratch_shapes=scratch,
            compiler_params=pltpu.CompilerParams(
                collective_id=0, has_side_effects=True, vmem_limit_bytes=60 * 2 ** 20
            ),
            cost_estimate=pl.CostEstimate(
                flops=units * 4 * tok * tok * DH,
                bytes_accessed=8 * query.size,
                transcendentals=units * tok * tok,
            ),
        )(pair_keys, pair_count, query, keys_in, values_in)

    tokens = P("ctx", "head", None)
    return jax.shard_map(
        body,
        mesh=mesh,
        in_specs=(tokens, tokens, tokens, P("ctx", None), P("ctx")),
        out_specs=tokens,
        check_vma=False,
    )
```
